1024 devices in a mesh: expert: 64 (over z_hi, x, core), tensor: 8 (over y), dp: 2 (over z_lo).
Axes of the slice: x: 8, y: 8, z: 8 (z_hi: 4, z_lo: 2; z = z_hi * 2 + z_lo), core: 2. Of those that a mesh axis runs over, the one named last changes fastest.
Arguments:
- grad_out: bfloat16 [16384, 3584], P('expert', ('tensor', 'dp')), may hold values from -16 to 16
- routes: int32 [16384, 2], P('expert'), may hold values from 0 to 63, all different within a row; in each aligned block of 256 rows (0 to 255, 256 to 511, ...) at most 12 rows name the same one
- probs: float32 [16384, 2], P('expert'), may hold values from 0.1 to 1
- expert_down: bfloat16 [64, 2432, 3584], P('expert', ('tensor', 'dp')), may hold values from -0.09375 to 0.09375
- expert_saved: bfloat16 [64, 2, 768, 2432], P('expert', None, None, ('tensor', 'dp')), may hold values from -4 to 4
- dense_down: bfloat16 [2432, 3584], P(('tensor', 'dp')), may hold values from -0.09375 to 0.09375
- dense_saved: bfloat16 [2, 16384, 2432], P(None, 'expert', ('tensor', 'dp')), may hold values from -4 to 4
Outputs:
- expert_pre_grad: bfloat16 [64, 2, 768, 2432], P('expert', None, None, ('tensor', 'dp'))
- expert_down_grad: bfloat16 [64, 2432, 3584], P('expert', ('tensor', 'dp'))
- dense_pre_grad: bfloat16 [2, 16384, 2432], P(None, 'expert', ('tensor', 'dp'))
- dense_down_grad: bfloat16 [2432, 3584], P(('tensor', 'dp'), 'expert')
The draws below stay inside these ranges and needn't reach their ends.
Inputs may be any that keep to these rules, and one draw needn't show every extreme that they name: `routes`: within each aligned block of 256 tokens (one group) no expert is named by more than 12 tokens, and in some block one expert is named by exactly 12; the two experts of a token differ.
All inputs are finite; a program needn't handle non-finite values.
Results may differ from the reference program's by a relative error of at most 0.0057.
Values may be sent and summed in bfloat16 or wider, within the bound.
No kernel may reach another device: no remote copies, remote signals or barrier semaphores. Data moves between devices by JAX's collectives and lax.ppermute only.
A program may use at most 64 MiB of HBM per device.

```python
import math
import jax
import jax.numpy as jnp
import numpy as np
from jax import lax

D = 3584
HE = 2432
HD = 2432
TOK_GRP = 256
EXPERTS = 64
CAP = 12
SLOTS = 768
TOKENS = 16384


def with_spikes(drawn, key, source, target, blocks, factor):
    owner, partner = [(jnp.arange(drawn.shape[dim]) // (drawn.shape[dim] // blocks)).reshape([-1 if axis == dim else 1 for axis in range(drawn.ndim)]) for dim in (source, target)]
    chosen = jax.random.permutation(key, blocks)[partner]
    strong = (owner == chosen) | (owner == (partner + blocks // 2) % blocks)
    return jnp.where(strong, factor * drawn, drawn)


def block_scale(rng, dims, shards, smallest, largest):
    def one(dim, parts):
        heights = jax.random.uniform(jax.random.fold_in(jax.random.fold_in(rng, 6), dim), (parts,), jnp.float32, smallest / len(shards), largest / len(shards))
        return jnp.repeat(jnp.exp(heights), dims[dim] // parts).reshape((-1,) + (1,) * (len(dims) - dim - 1))

    loudness = one(*shards[0])
    for cut in shards[1:]:
        loudness = loudness * one(*cut)
    return loudness


def assign_block(own_key, own, number, rows, amount, top, limit, lean):
    order = jax.random.permutation(own_key, amount)
    crowded, ordinary = portions_of(amount, rows * top, limit, lean, True), portions_of(amount, rows * top, limit, lean, False)
    places = jnp.arange(amount)

    def named(sizes, turn):
        used = int((sizes > 0).sum())
        fixed = max(1, used // 4)
        shifted = fixed + (places - fixed + turn * (used - fixed)) % max(1, amount - fixed)
        return jnp.zeros((amount,), jnp.int32).at[order[jnp.where(places < fixed, places, shifted)]].set(jnp.asarray(sizes, jnp.int32))

    sizes = jnp.where(number % 4 == 0, named(crowded, number // 4), named(ordinary, number - number // 4 - 1))
    mixed = jax.random.permutation(jax.random.fold_in(own, 3), amount)
    donor, receiver = mixed[0:amount // 2 * 2:2], mixed[1:amount // 2 * 2:2]
    slack = jnp.minimum(sizes[donor] - 1, limit - sizes[receiver]) // 2
    slack = jnp.where((donor == order[0]) | (receiver == order[0]) | (sizes[receiver] == 0), 0, jnp.maximum(slack, 0))
    shifted = jax.random.randint(jax.random.fold_in(own, 4), (amount // 2,), 0, 1 << 20) % (slack + 1)
    sizes = sizes.at[donor].add(-shifted).at[receiver].add(shifted)
    items = jnp.searchsorted(jnp.cumsum(sizes), jnp.arange(rows * top), side="right").astype(jnp.int32)
    listing = items.reshape(top, rows).T
    listing = listing[jax.random.permutation(jax.random.fold_in(own, 1), rows)]
    turn = jax.random.randint(jax.random.fold_in(own, 2), (rows, 1), 0, top)
    return jnp.take_along_axis(listing, (jnp.arange(top)[None, :] + turn) % top, axis=1)


def portions_of(number_of, total, most, slope, full):
    portions = [(1 << 20) // math.isqrt(standing ** slope) + 1 for standing in range(1, number_of + 1)]
    largest = most if full else min(most, max(-(-total // number_of), total * portions[0] // sum(portions)))
    least = 1 if total - largest >= number_of - 1 else 0
    given, rest = [largest] + [least] * (number_of - 1), total - largest - least * (number_of - 1)
    while rest > 0:
        candidates = [i for i in range(1, number_of) if given[i] < largest] or [i for i in range(1, number_of) if given[i] < most]
        whole, remaining = sum([portions[i] for i in candidates]), rest
        for i in candidates:
            extra = min(most - given[i], max(1, remaining * portions[i] // whole), rest)
            given[i] = given[i] + extra
            rest = rest - extra
    return np.array(given)


def centred(key, shape, scale, limit, split=(), kind=jnp.bfloat16):
    entries = jax.random.normal(key, shape, jnp.float32) * scale
    if len(split) > 0:
        entries = block_scale(key, shape, split, -0.22, 0.18) * entries
    return jnp.clip(entries, min=-limit, max=limit).astype(kind)


def noise_with(own_key, dims, deviation, limit, split, heavy, held_as=jnp.bfloat16):
    entries = deviation * jax.random.normal(own_key, dims, jnp.float32)
    if split:
        entries = entries * block_scale(own_key, dims, split, -0.22, 0.18)
    return jnp.clip(with_spikes(entries, jax.random.fold_in(own_key, 3), *heavy), -limit, limit).astype(held_as)


def setup_inputs(seed: int = 0) -> dict:
    streams_of = jax.random.split(jax.random.key(seed), 8)
    grad_out = noise_with(streams_of[0], (TOKENS, D), 1.0, 16.0, ((0, 64), (1, 16)), (0, 1, 64, 4.0))
    routes_keys = jax.random.split(jax.random.fold_in(streams_of[1], 1), TOKENS // TOK_GRP)
    routes_turns = jax.random.permutation(jax.random.fold_in(streams_of[1], 3), TOKENS // TOK_GRP)
    routes = jax.vmap(lambda own, number: assign_block(jax.random.fold_in(streams_of[1], 2), own, number, TOK_GRP, EXPERTS, 2, CAP, 2))(routes_keys, routes_turns).reshape((TOKENS, 2))
    probs = jnp.clip(0.1 + 0.9 * jax.random.uniform(streams_of[2], (TOKENS, 2), jnp.float32) ** block_scale(streams_of[2], (TOKENS, 2), ((0, 64),), -0.2, 0.2), 0.1, 1.0)
    expert_down = centred(streams_of[3], (EXPERTS, HE, D), D ** -0.5, 0.09375, ((0, 64), (1, 16)))
    expert_saved = centred(streams_of[4], (EXPERTS, 2, SLOTS, HE), 1.0, 4.0, ((0, 64), (3, 16)))
    dense_down = centred(streams_of[5], (HD, D), D ** -0.5, 0.09375, ((0, 16),))
    dense_saved = centred(streams_of[6], (2, TOKENS, HD), 1.0, 4.0, ((1, 64), (2, 16)))
    return dict(grad_out=grad_out, routes=routes, probs=probs, expert_down=expert_down, expert_saved=expert_saved, dense_down=dense_down, dense_saved=dense_saved)


def slot_numbers(routes_group, expert_count, capacity):
    flat_routes = routes_group.reshape(-1)
    experts_row = jnp.arange(expert_count, dtype=jnp.int32)
    onehot = (flat_routes[:, None] == experts_row[None, :]).astype(jnp.int32)
    before = (jnp.cumsum(onehot, axis=0) - onehot).astype(jnp.int32)
    position = jnp.sum(before * onehot, axis=1).astype(jnp.int32)
    return (flat_routes * capacity + position).astype(jnp.int32).reshape(routes_group.shape)


def dispatch_table(routes_group, probs_group, expert_count, capacity):
    slots_here = slot_numbers(routes_group, expert_count, capacity)
    targets = jnp.arange(expert_count * capacity, dtype=jnp.int32)
    match = slots_here[None, :, :] == targets[:, None, None]
    return jnp.sum(jnp.where(match, probs_group[None, :, :], jnp.float32(0.0)), axis=2)


def swiglu_parts(saved_pair):
    gate_pre = saved_pair[0].astype(jnp.float32)
    up_pre = saved_pair[1].astype(jnp.float32)
    sigmoid_gate = jax.nn.sigmoid(gate_pre)
    hidden = (gate_pre * sigmoid_gate * up_pre).astype(jnp.bfloat16)
    return gate_pre, up_pre, sigmoid_gate, hidden


def pre_cotangents(hidden_cot, gate_pre, up_pre, sigmoid_gate):
    gate_cot = hidden_cot * up_pre * sigmoid_gate * (1.0 + gate_pre * (1.0 - sigmoid_gate))
    up_cot = hidden_cot * gate_pre * sigmoid_gate
    return jnp.stack([gate_cot, up_cot]).astype(jnp.bfloat16)


def reference(grad_out, routes, probs, expert_down, expert_saved, dense_down, dense_saved):
    groups = TOKENS // TOK_GRP
    grad_groups = grad_out.reshape(groups, TOK_GRP, D)
    route_groups = routes.reshape(groups, TOK_GRP, 2)
    prob_groups = probs.reshape(groups, TOK_GRP, 2)

    def one_group(packed):
        rows, route_rows, prob_rows = packed
        table = dispatch_table(route_rows, prob_rows, EXPERTS, CAP)
        return jnp.dot(table, rows.astype(jnp.float32), precision=lax.Precision.HIGHEST).astype(jnp.bfloat16)

    sent = lax.map(one_group, (grad_groups, route_groups, prob_groups))
    sent = sent.reshape(groups, EXPERTS, CAP, D).transpose(1, 0, 2, 3).reshape(EXPERTS, SLOTS, D)

    def one_expert(packed):
        sent_rows, down_rows, saved_pair = packed
        gate_pre, up_pre, sigmoid_gate, hidden = swiglu_parts(saved_pair)
        hidden_cot = jnp.dot(sent_rows, down_rows.T, preferred_element_type=jnp.float32)
        pre_grad = pre_cotangents(hidden_cot, gate_pre, up_pre, sigmoid_gate)
        down_grad = jnp.dot(hidden.T, sent_rows, preferred_element_type=jnp.float32).astype(jnp.bfloat16)
        return pre_grad, down_grad

    expert_pre_grad, expert_down_grad = lax.map(one_expert, (sent, expert_down, expert_saved))

    gate_pre, up_pre, sigmoid_gate, dense_hidden = swiglu_parts(dense_saved)
    dense_cot = jnp.dot(grad_out, dense_down.T, preferred_element_type=jnp.float32)
    dense_pre_grad = pre_cotangents(dense_cot, gate_pre, up_pre, sigmoid_gate)
    dense_down_grad = jnp.dot(dense_hidden.T, grad_out, preferred_element_type=jnp.float32).astype(jnp.bfloat16)
    return expert_pre_grad, expert_down_grad, dense_pre_grad, dense_down_grad
```

```python
import jax
import jax.numpy as jnp
from jax import lax
from jax.sharding import Mesh, PartitionSpec as P

BF = jnp.bfloat16
F32 = jnp.float32
EXPERT = ("zh", "x", "core")
SHARE = ("y", "zl")


def slot_numbers(routes_group, expert_count, capacity):
    flat_routes = routes_group.reshape(-1)
    experts_row = jnp.arange(expert_count, dtype=jnp.int32)
    onehot = (flat_routes[:, None] == experts_row[None, :]).astype(jnp.int32)
    before = jnp.cumsum(onehot, axis=0) - onehot
    position = jnp.sum(before * onehot, axis=1)
    return (flat_routes * capacity + position).reshape(routes_group.shape)


def dispatch_table(routes_group, probs_group, expert_count, capacity):
    slots_here = slot_numbers(routes_group, expert_count, capacity)
    targets = jnp.arange(expert_count * capacity, dtype=jnp.int32)
    match = slots_here[None, :, :] == targets[:, None, None]
    return jnp.sum(jnp.where(match, probs_group[None, :, :], jnp.float32(0.0)), axis=2)


def swiglu_parts(saved_pair):
    gate_pre = saved_pair[0].astype(F32)
    up_pre = saved_pair[1].astype(F32)
    sigmoid_gate = jax.nn.sigmoid(gate_pre)
    hidden = (gate_pre * sigmoid_gate * up_pre).astype(BF)
    return (gate_pre, up_pre, sigmoid_gate, hidden)


def pre_cotangents(hidden_cot, gate_pre, up_pre, sigmoid_gate):
    gate_cot = hidden_cot * up_pre * sigmoid_gate * (1.0 + gate_pre * (1.0 - sigmoid_gate))
    up_cot = hidden_cot * gate_pre * sigmoid_gate
    return jnp.stack([gate_cot, up_cot]).astype(BF)


def gather_features(columns):
    other = lax.ppermute(columns, "zl", [(0, 1), (1, 0)])
    first = lax.axis_index("zl") == 0
    pair = jnp.stack([jnp.where(first, columns, other), jnp.where(first, other, columns)])
    whole = lax.all_gather(pair, "y", axis=0, tiled=False)
    return whole.reshape(-1, columns.shape[1])


def scatter_sum(terms):
    parts = lax.axis_size(EXPERT)
    width, hidden = terms.shape[0] // parts, terms.shape[1]
    blocks = terms.astype(BF).reshape(parts, width, hidden)
    whole = hidden // 128 * 128
    tail = blocks[:, :, whole:].reshape(parts, width * (hidden - whole))
    tail_rows = -(-tail.shape[1] // 128)
    tail = jnp.pad(tail, ((0, 0), (0, tail_rows * 128 - tail.shape[1]))).reshape(parts, tail_rows, 128)
    packed = jnp.concatenate([blocks[:, :, :whole].reshape(parts, -1, 128), tail], axis=1)
    came = lax.all_to_all(packed, EXPERT, split_axis=0, concat_axis=0, tiled=True)
    total = jnp.sum(came.astype(F32), axis=0)
    head_rows = width * whole // 128
    head = total[:head_rows].reshape(width, whole)
    tail = total[head_rows:].reshape(-1)[: width * (hidden - whole)].reshape(width, hidden - whole)
    return jnp.concatenate([head, tail], axis=1)


def body(grad_out, routes, probs, expert_down, expert_saved, dense_down, dense_saved):
    expert_count = lax.axis_size(EXPERT)
    capacity = expert_saved.shape[2] // expert_count
    feature_width = grad_out.shape[1]
    down_local = expert_down[0]

    grad_whole = gather_features(grad_out.T)

    table = dispatch_table(routes, probs, expert_count, capacity)
    outgoing = jnp.dot(table, grad_out.astype(F32), precision=lax.Precision.HIGHEST).astype(BF)
    outgoing = outgoing.reshape(expert_count, capacity * feature_width // 128, 128)
    received = lax.all_to_all(outgoing, EXPERT, split_axis=0, concat_axis=0, tiled=True)
    received = received.reshape(expert_count * capacity, feature_width)
    sent = gather_features(received.T)

    gate_dense, up_dense, sigmoid_dense, dense_hidden = swiglu_parts(dense_saved)
    dense_terms = jnp.einsum("fr,rh->fh", grad_whole, dense_hidden, preferred_element_type=F32)
    dense_share = scatter_sum(dense_terms)
    dense_cot = jnp.einsum("fr,hf->rh", grad_whole, dense_down, preferred_element_type=F32)

    gate_expert, up_expert, sigmoid_expert, expert_hidden = swiglu_parts(expert_saved[0])
    expert_cot = jnp.einsum("fr,hf->rh", sent, down_local, preferred_element_type=F32)
    expert_grad = jnp.einsum("rh,fr->hf", expert_hidden, sent, preferred_element_type=F32)

    expert_pre_grad = pre_cotangents(expert_cot, gate_expert, up_expert, sigmoid_expert)[None]
    expert_down_grad = expert_grad.astype(BF)[None]
    dense_pre_grad = pre_cotangents(dense_cot, gate_dense, up_dense, sigmoid_dense)
    dense_down_grad = dense_share.T.astype(BF)
    return (expert_pre_grad, expert_down_grad, dense_pre_grad, dense_down_grad)


def solution(mesh):
    experts, tensors, pairs = mesh.devices.shape
    chips = min(8, experts // 2)
    fine = Mesh(
        mesh.devices.reshape(experts // (2 * chips), chips, 2, tensors, pairs),
        EXPERT + SHARE,
    )
    return jax.shard_map(
        body,
        mesh=fine,
        in_specs=(
            P(EXPERT, SHARE),
            P(EXPERT, None),
            P(EXPERT, None),
            P(EXPERT, SHARE, None),
            P(EXPERT, None, None, SHARE),
            P(SHARE, None),
            P(None, EXPERT, SHARE),
        ),
        out_specs=(
            P(EXPERT, None, None, SHARE),
            P(EXPERT, SHARE, None),
            P(None, EXPERT, SHARE),
            P(SHARE, EXPERT),
        ),
        check_vma=False,
    )
```

```python
import functools

import jax
import jax.numpy as jnp
from jax import lax
from jax.experimental import pallas as pl
from jax.experimental.pallas import tpu as pltpu
from jax.sharding import Mesh, PartitionSpec as P

BF = jnp.bfloat16
F32 = jnp.float32
EXPERT = ("zh", "x", "core")
SHARE = ("y", "zl")
LANES = 128
VMEM_LIMIT = 48 * 1024 * 1024


def local_kernel(kernel, outs, flops, moved, scalars=0, arrays=1):
    specs = [pl.BlockSpec(memory_space=pltpu.SMEM)] * scalars
    return pl.pallas_call(
        kernel,
        out_shape=outs,
        in_specs=specs + [pl.BlockSpec(memory_space=pltpu.VMEM)] * arrays,
        compiler_params=pltpu.CompilerParams(vmem_limit_bytes=VMEM_LIMIT),
        cost_estimate=pl.CostEstimate(flops=flops, bytes_accessed=moved, transcendentals=0),
    )


def dispatch_kernel(experts, capacity, routes_ref, probs_ref, grad_ref, out_ref):
    tokens, features = routes_ref.shape[1], grad_ref.shape[0]
    rows = out_ref.shape[0]
    first, second = routes_ref[0:1, :], routes_ref[1:2, :]
    names = lax.broadcasted_iota(jnp.int32, (experts, tokens), 0)
    on_first, on_second = names == first, names == second
    named = (on_first | on_second).astype(F32).astype(BF)
    earlier = lax.broadcasted_iota(jnp.int32, (tokens, tokens), 0) < lax.broadcasted_iota(
        jnp.int32, (tokens, tokens), 1
    )
    before = jnp.dot(named, earlier.astype(F32).astype(BF), preferred_element_type=F32)
    place_first = jnp.sum(jnp.where(on_first, before, 0.0), axis=0, keepdims=True)
    place_second = jnp.sum(jnp.where(on_second, before, 0.0), axis=0, keepdims=True)
    slot_first = first * capacity + place_first.astype(jnp.int32)
    slot_second = second * capacity + place_second.astype(jnp.int32)
    step = rows // 4
    for part in range(4):
        row = lax.broadcasted_iota(jnp.int32, (step, 1), 0) + part * step
        slot = row // (2 * capacity) * capacity + row % capacity
        is_first, is_second = slot == slot_first, slot == slot_second
        table = jnp.where(is_first, probs_ref[0:1, :], jnp.where(is_second, probs_ref[1:2, :], 0.0))
        weight = jnp.sum(table, axis=1, keepdims=True)
        onehot = (is_first | is_second).astype(F32).astype(BF)
        picked = lax.dot_general(
            onehot, grad_ref[...], (((1,), (1,)), ((), ())), preferred_element_type=F32
        )
        sent = picked * weight
        low = sent[:, :LANES]
        high = jnp.concatenate(
            [sent[:, LANES:], jnp.zeros((step, 2 * LANES - features), F32)], axis=1
        )
        out_ref[part * step : (part + 1) * step, :] = jnp.where(
            row % (2 * capacity) < capacity, low, high
        ).astype(BF)


def arrange_kernel(capacity, came_ref, out_ref):
    rows, features, slots = came_ref.shape[0], out_ref.shape[0], out_ref.shape[1]
    parts = 2
    row_step, slot_step = rows // parts, slots // parts
    row = lax.broadcasted_iota(jnp.int32, (row_step, 1), 0)
    slot = lax.broadcasted_iota(jnp.int32, (1, slot_step), 1)
    wanted = slot // capacity * (2 * capacity) + slot % capacity
    for half in range(2):
        pick = (row == wanted + half * capacity).astype(F32).astype(BF)
        for part in range(parts):
            block = came_ref[part * row_step : (part + 1) * row_step, :]
            value = lax.dot_general(
                block, pick, (((0,), (0,)), ((), ())), preferred_element_type=F32
            ).astype(BF)
            top = min(features - half * LANES, LANES)
            out_ref[half * LANES : half * LANES + top, part * slot_step : (part + 1) * slot_step] = value[
                :top, :
            ]


def split_kernel(runs, half_ref, dense_ref, expert_ref, mine_ref, theirs_ref):
    width = dense_ref.shape[1] // (2 * runs)

    def columns(ref, half):
        return jnp.concatenate(
            [ref[:, (2 * run + half) * width : (2 * run + half + 1) * width] for run in range(runs)], axis=1
        )

    for half in range(2):

        @pl.when(half_ref[0] == half)
        def _():
            for index, ref in enumerate((dense_ref, expert_ref)):
                mine_ref[index] = columns(ref, half)
                theirs_ref[index] = columns(ref, 1 - half)


def join_kernel(runs, half_ref, own_ref, other_ref, out_ref):
    width = own_ref.shape[1] // runs

    def joined(low_ref, high_ref):
        pieces = []
        for run in range(runs):
            for ref in (low_ref, high_ref):
                pieces.append(ref[:, run * width : (run + 1) * width])
        return jnp.concatenate(pieces, axis=1)

    @pl.when(half_ref[0] == 0)
    def _():
        out_ref[...] = joined(own_ref, other_ref)

    @pl.when(half_ref[0] == 1)
    def _():
        out_ref[...] = joined(other_ref, own_ref)


def swiglu_parts(gate_saved, up_saved):
    gate_pre = gate_saved.astype(F32)
    up_pre = up_saved.astype(F32)
    sigmoid_gate = jax.nn.sigmoid(gate_pre)
    hidden = (gate_pre * sigmoid_gate * up_pre).astype(BF)
    return (gate_pre, up_pre, sigmoid_gate, hidden)


def pre_cotangents(hidden_cot, gate_pre, up_pre, sigmoid_gate):
    gate_cot = hidden_cot * up_pre * sigmoid_gate * (1.0 + gate_pre * (1.0 - sigmoid_gate))
    up_cot = hidden_cot * gate_pre * sigmoid_gate
    return jnp.stack([gate_cot, up_cot]).astype(BF)


def after(values, earlier):
    return lax.optimization_barrier((values, earlier))[0]


def swap(values):
    return lax.ppermute(values, "zl", [(0, 1), (1, 0)])


def gather_columns(rows):
    whole = lax.all_gather(rows, "y", axis=0, tiled=False)
    return whole.reshape(-1, rows.shape[1])


def terms_kernel(runs, grad_ref, first_ref, second_ref, out_ref):
    parts, rows, _ = out_ref.shape
    hidden, width = first_ref.shape[0], grad_ref.shape[0] * 2 // parts
    span = parts // (2 * runs)
    stack, extra = rows - width, hidden - LANES
    for run in range(runs):
        grads = grad_ref[run * span * width : (run + 1) * span * width, :]
        for half, ref in enumerate((first_ref, second_ref)):
            value = lax.dot_general(
                grads, ref[...], (((1,), (1,)), ((), ())), preferred_element_type=F32
            )
            for index in range(span):
                block = value[index * width : (index + 1) * width, :]
                last = jnp.concatenate(
                    [block[:, LANES:], jnp.zeros((-width % stack, extra), F32)], axis=0
                )
                count = last.shape[0] // stack
                last = jnp.concatenate(
                    [last[piece * stack : (piece + 1) * stack, :] for piece in range(count)]
                    + [jnp.zeros((stack, LANES - count * extra), F32)],
                    axis=1,
                )
                out_ref[(run * 2 + half) * span + index] = jnp.concatenate(
                    [block[:, :LANES], last], axis=0
                ).astype(BF)


def total_kernel(came_ref, out_ref):
    parts, rows, _ = came_ref.shape
    width, hidden = out_ref.shape
    stack, extra = rows - width, hidden - LANES
    total = came_ref[0].astype(F32)
    for part in range(1, parts):
        total = total + came_ref[part].astype(F32)
    last = jnp.concatenate(
        [total[width:, piece * extra : (piece + 1) * extra] for piece in range(-(-width // stack))], axis=0
    )
    out_ref[...] = jnp.concatenate([total[:width, :], last[:width, :]], axis=1).astype(BF)


def scatter_terms(grad_half, units):
    parts, runs = lax.axis_size(EXPERT), lax.axis_size("y")
    width, hidden = grad_half.shape[0] * 2 // parts, units[0].shape[0]
    return local_kernel(
        functools.partial(terms_kernel, runs),
        jax.ShapeDtypeStruct((parts, width + 16, LANES), BF),
        4 * grad_half.shape[0] * hidden * grad_half.shape[1],
        4 * parts * width * LANES,
        0,
        3,
    )(grad_half, *units)


def scatter_total(came, width, hidden):
    mine = local_kernel(
        total_kernel, jax.ShapeDtypeStruct((width, hidden), BF), came.size, 2 * came.size
    )(came)
    chips = lax.axis_size("x")
    route = [(2 * x + z, 2 * (x ^ 2) + (1 - z)) for x in range(chips) for z in range(2)]
    other = lax.ppermute(mine, ("x", "zl"), route)
    here = lax.axis_index("x") // 2 % 2 == lax.axis_index("zl")
    return jnp.where(here, mine, other)


def body(grad_out, routes, probs, expert_down, expert_saved, dense_down, dense_saved):
    expert_count, runs = lax.axis_size(EXPERT), lax.axis_size("y")
    slots, hidden_count = expert_saved.shape[2:]
    capacity = slots // expert_count
    tokens, feature_width = grad_out.shape
    model_width = dense_down.shape[1]
    half = lax.axis_index("zl").astype(jnp.int32)
    half_index = half.reshape(1)
    grad_rows = grad_out.T

    grad_half = gather_columns(grad_rows)

    outgoing = local_kernel(
        functools.partial(dispatch_kernel, expert_count, capacity),
        jax.ShapeDtypeStruct((expert_count * 2 * capacity, LANES), BF),
        4 * slots * tokens * feature_width,
        4 * slots * LANES,
        arrays=3,
    )(routes.T, probs.T, grad_rows)
    outgoing = outgoing.reshape(expert_count, 2 * capacity, LANES)
    received = lax.all_to_all(outgoing, EXPERT, split_axis=0, concat_axis=0, tiled=True)
    received = local_kernel(
        functools.partial(arrange_kernel, capacity),
        jax.ShapeDtypeStruct((feature_width, slots), BF),
        4 * slots * slots * LANES,
        8 * slots * LANES,
    )(received.reshape(-1, LANES))
    sent_half = gather_columns(received)

    dense_saved, expert_saved, dense_down, expert_down = after(
        (dense_saved, expert_saved, dense_down, expert_down), received
    )
    gate_dense, up_dense, sigmoid_dense, dense_units = swiglu_parts(dense_saved[0].T, dense_saved[1].T)
    gate_expert, up_expert, sigmoid_expert, expert_units = swiglu_parts(
        expert_saved[0, 0].T, expert_saved[0, 1].T
    )
    units_other = swap(jnp.concatenate([dense_units, expert_units], axis=1))
    dense_units_other, expert_units_other = units_other[:, :tokens], units_other[:, tokens:]
    weights = jax.ShapeDtypeStruct((2, hidden_count, model_width // 2), BF)
    mine, theirs = local_kernel(
        functools.partial(split_kernel, runs), [weights, weights], 0, 8 * hidden_count * model_width, 1, 2
    )(half_index, dense_down, expert_down[0])
    theirs = swap(theirs)

    first = half == 0
    units = (jnp.where(first, dense_units, dense_units_other), jnp.where(first, dense_units_other, dense_units))
    terms = scatter_terms(grad_half, units)
    came = lax.all_to_all(terms, EXPERT, split_axis=0, concat_axis=0, tiled=True)
    dense_share = scatter_total(came, model_width // expert_count, hidden_count)
    grad_half = after(grad_half, terms)
    cot_other = jnp.einsum("hf,fr->hr", theirs[0], grad_half, preferred_element_type=F32)
    cot_own = jnp.einsum("hf,fr->hr", mine[0], grad_half, preferred_element_type=F32)
    dense_cot = cot_own + swap(cot_other.astype(BF)).astype(F32)

    sent_half = after(sent_half, came)
    grad_other = jnp.einsum("hr,fr->hf", expert_units_other, sent_half, preferred_element_type=F32)
    grad_other = grad_other.astype(BF)
    sent_half = after(sent_half, grad_other)
    grad_other = swap(grad_other)
    cot_other = jnp.einsum("hf,fr->hr", theirs[1], sent_half, preferred_element_type=F32)
    cot_other = cot_other.astype(BF)
    sent_half = after(sent_half, cot_other)
    cot_other = swap(cot_other)
    grad_own = jnp.einsum("hr,fr->hf", expert_units, sent_half, preferred_element_type=F32).astype(BF)
    cot_own = jnp.einsum("hf,fr->hr", mine[1], sent_half, preferred_element_type=F32)
    expert_cot = cot_own + cot_other.astype(F32)
    expert_down_grad = local_kernel(
        functools.partial(join_kernel, runs),
        jax.ShapeDtypeStruct((hidden_count, model_width), BF),
        0,
        4 * hidden_count * model_width,
        1,
        2,
    )(half_index, grad_own, grad_other)[None]

    expert_pre_grad = pre_cotangents(expert_cot, gate_expert, up_expert, sigmoid_expert)
    expert_pre_grad = expert_pre_grad.transpose(0, 2, 1)[None]
    dense_pre_grad = pre_cotangents(dense_cot, gate_dense, up_dense, sigmoid_dense).transpose(0, 2, 1)
    dense_down_grad = dense_share.T
    return (expert_pre_grad, expert_down_grad, dense_pre_grad, dense_down_grad)


def solution(mesh):
    experts, tensors, pairs = mesh.devices.shape
    chips = min(8, experts // 2)
    fine = Mesh(
        mesh.devices.reshape(experts // (2 * chips), chips, 2, tensors, pairs),
        EXPERT + SHARE,
    )
    return jax.shard_map(
        body,
        mesh=fine,
        in_specs=(
            P(EXPERT, SHARE),
            P(EXPERT, None),
            P(EXPERT, None),
            P(EXPERT, SHARE, None),
            P(EXPERT, None, None, SHARE),
            P(SHARE, None),
            P(None, EXPERT, SHARE),
        ),
        out_specs=(
            P(EXPERT, None, None, SHARE),
            P(EXPERT, SHARE, None),
            P(None, EXPERT, SHARE),
            P(SHARE, EXPERT),
        ),
        check_vma=False,
    )
```

```python
import functools

import jax
import jax.numpy as jnp
from jax import lax
from jax.experimental import pallas as pl
from jax.experimental.pallas import tpu as pltpu
from jax.sharding import Mesh, PartitionSpec as P

BF = jnp.bfloat16
F32 = jnp.float32
EXPERT = ("zh", "x", "core")
SHARE = ("y", "zl")
LANES = 128
VMEM_LIMIT = 48 * 1024 * 1024


def local_kernel(kernel, outs, flops, moved, scalars=0, arrays=1):
    specs = [pl.BlockSpec(memory_space=pltpu.SMEM)] * scalars
    return pl.pallas_call(
        kernel,
        out_shape=outs,
        in_specs=specs + [pl.BlockSpec(memory_space=pltpu.VMEM)] * arrays,
        compiler_params=pltpu.CompilerParams(vmem_limit_bytes=VMEM_LIMIT),
        cost_estimate=pl.CostEstimate(flops=flops, bytes_accessed=moved, transcendentals=0),
    )


def dispatch_kernel(experts, capacity, routes_ref, probs_ref, grad_ref, out_ref):
    tokens, features = routes_ref.shape[1], grad_ref.shape[0]
    rows = out_ref.shape[0]
    first, second = routes_ref[0:1, :], routes_ref[1:2, :]
    names = lax.broadcasted_iota(jnp.int32, (experts, tokens), 0)
    on_first, on_second = names == first, names == second
    named = (on_first | on_second).astype(F32).astype(BF)
    earlier = lax.broadcasted_iota(jnp.int32, (tokens, tokens), 0) < lax.broadcasted_iota(
        jnp.int32, (tokens, tokens), 1
    )
    before = jnp.dot(named, earlier.astype(F32).astype(BF), preferred_element_type=F32)
    place_first = jnp.sum(jnp.where(on_first, before, 0.0), axis=0, keepdims=True)
    place_second = jnp.sum(jnp.where(on_second, before, 0.0), axis=0, keepdims=True)
    slot_first = first * capacity + place_first.astype(jnp.int32)
    slot_second = second * capacity + place_second.astype(jnp.int32)
    step = rows // 4
    for part in range(4):
        row = lax.broadcasted_iota(jnp.int32, (step, 1), 0) + part * step
        slot = row // (2 * capacity) * capacity + row % capacity
        is_first, is_second = slot == slot_first, slot == slot_second
        table = jnp.where(is_first, probs_ref[0:1, :], jnp.where(is_second, probs_ref[1:2, :], 0.0))
        weight = jnp.sum(table, axis=1, keepdims=True)
        onehot = (is_first | is_second).astype(F32).astype(BF)
        picked = lax.dot_general(
            onehot, grad_ref[...], (((1,), (1,)), ((), ())), preferred_element_type=F32
        )
        sent = picked * weight
        low = sent[:, :LANES]
        high = jnp.concatenate(
            [sent[:, LANES:], jnp.zeros((step, 2 * LANES - features), F32)], axis=1
        )
        out_ref[part * step : (part + 1) * step, :] = jnp.where(
            row % (2 * capacity) < capacity, low, high
        ).astype(BF)


def arrange_kernel(capacity, came_ref, out_ref):
    rows, features, slots = came_ref.shape[0], out_ref.shape[0], out_ref.shape[1]
    parts = 2
    row_step, slot_step = rows // parts, slots // parts
    row = lax.broadcasted_iota(jnp.int32, (row_step, 1), 0)
    slot = lax.broadcasted_iota(jnp.int32, (1, slot_step), 1)
    wanted = slot // capacity * (2 * capacity) + slot % capacity
    for half in range(2):
        pick = (row == wanted + half * capacity).astype(F32).astype(BF)
        for part in range(parts):
            block = came_ref[part * row_step : (part + 1) * row_step, :]
            value = lax.dot_general(
                block, pick, (((0,), (0,)), ((), ())), preferred_element_type=F32
            ).astype(BF)
            top = min(features - half * LANES, LANES)
            out_ref[half * LANES : half * LANES + top, part * slot_step : (part + 1) * slot_step] = value[
                :top, :
            ]


def split_kernel(runs, half_ref, weights_ref, mine_ref, theirs_ref):
    width = weights_ref.shape[1] // (2 * runs)

    def columns(half):
        return jnp.concatenate(
            [weights_ref[:, (2 * run + half) * width : (2 * run + half + 1) * width] for run in range(runs)],
            axis=1,
        )

    for half in range(2):

        @pl.when(half_ref[0] == half)
        def _():
            mine_ref[...] = columns(half)
            theirs_ref[...] = columns(1 - half)


def join_kernel(runs, half_ref, own_ref, other_ref, out_ref):
    width = own_ref.shape[1] // runs

    def joined(low_ref, high_ref):
        pieces = []
        for run in range(runs):
            for ref in (low_ref, high_ref):
                pieces.append(ref[:, run * width : (run + 1) * width])
        return jnp.concatenate(pieces, axis=1)

    @pl.when(half_ref[0] == 0)
    def _():
        out_ref[...] = joined(own_ref, other_ref)

    @pl.when(half_ref[0] == 1)
    def _():
        out_ref[...] = joined(other_ref, own_ref)


def swiglu_parts(gate_saved, up_saved):
    gate_pre = gate_saved.astype(F32)
    up_pre = up_saved.astype(F32)
    sigmoid_gate = jax.nn.sigmoid(gate_pre)
    hidden = (gate_pre * sigmoid_gate * up_pre).astype(BF)
    return (gate_pre, up_pre, sigmoid_gate, hidden)


def pre_cotangents(hidden_cot, gate_pre, up_pre, sigmoid_gate):
    gate_cot = hidden_cot * up_pre * sigmoid_gate * (1.0 + gate_pre * (1.0 - sigmoid_gate))
    up_cot = hidden_cot * gate_pre * sigmoid_gate
    return jnp.stack([gate_cot, up_cot]).astype(BF)


def after(values, earlier):
    return lax.optimization_barrier((values, earlier))[0]


def swap(values):
    return lax.ppermute(values, "zl", [(0, 1), (1, 0)])


def gather_columns(rows):
    whole = lax.all_gather(rows, "y", axis=0, tiled=False)
    return whole.reshape(-1, rows.shape[1])


def terms_kernel(runs, grad_ref, first_ref, second_ref, out_ref):
    parts, rows, _ = out_ref.shape
    hidden, width = first_ref.shape[0], grad_ref.shape[0] * 2 // parts
    span = parts // (2 * runs)
    stack, extra = rows - width, hidden - LANES
    for run in range(runs):
        grads = grad_ref[run * span * width : (run + 1) * span * width, :]
        for half, ref in enumerate((first_ref, second_ref)):
            value = lax.dot_general(
                grads, ref[...], (((1,), (1,)), ((), ())), preferred_element_type=F32
            )
            for index in range(span):
                block = value[index * width : (index + 1) * width, :]
                last = jnp.concatenate(
                    [block[:, LANES:], jnp.zeros((-width % stack, extra), F32)], axis=0
                )
                count = last.shape[0] // stack
                last = jnp.concatenate(
                    [last[piece * stack : (piece + 1) * stack, :] for piece in range(count)]
                    + [jnp.zeros((stack, LANES - count * extra), F32)],
                    axis=1,
                )
                out_ref[(run * 2 + half) * span + index] = jnp.concatenate(
                    [block[:, :LANES], last], axis=0
                ).astype(BF)


def total_kernel(came_ref, out_ref):
    parts, rows, _ = came_ref.shape
    width, hidden = out_ref.shape
    stack, extra = rows - width, hidden - LANES
    total = came_ref[0].astype(F32)
    for part in range(1, parts):
        total = total + came_ref[part].astype(F32)
    last = jnp.concatenate(
        [total[width:, piece * extra : (piece + 1) * extra] for piece in range(-(-width // stack))], axis=0
    )
    out_ref[...] = jnp.concatenate([total[:width, :], last[:width, :]], axis=1).astype(BF)


def scatter_terms(grad_half, units):
    parts, runs = lax.axis_size(EXPERT), lax.axis_size("y")
    width, hidden = grad_half.shape[0] * 2 // parts, units[0].shape[0]
    return local_kernel(
        functools.partial(terms_kernel, runs),
        jax.ShapeDtypeStruct((parts, width + 16, LANES), BF),
        4 * grad_half.shape[0] * hidden * grad_half.shape[1],
        4 * parts * width * LANES,
        0,
        3,
    )(grad_half, *units)


def scatter_total(came, width, hidden):
    mine = local_kernel(
        total_kernel, jax.ShapeDtypeStruct((width, hidden), BF), came.size, 2 * came.size
    )(came)
    chips = lax.axis_size("x")
    route = [(2 * x + z, 2 * (x ^ 2) + (1 - z)) for x in range(chips) for z in range(2)]
    other = lax.ppermute(mine, ("x", "zl"), route)
    here = lax.axis_index("x") // 2 % 2 == lax.axis_index("zl")
    return jnp.where(here, mine, other)


def body(grad_out, routes, probs, expert_down, expert_saved, dense_down, dense_saved):
    expert_count, runs = lax.axis_size(EXPERT), lax.axis_size("y")
    slots, hidden_count = expert_saved.shape[2:]
    capacity = slots // expert_count
    tokens, feature_width = grad_out.shape
    model_width = dense_down.shape[1]
    half = lax.axis_index("zl").astype(jnp.int32)
    half_index = half.reshape(1)
    grad_rows = grad_out.T

    grad_half = gather_columns(grad_rows)

    outgoing = local_kernel(
        functools.partial(dispatch_kernel, expert_count, capacity),
        jax.ShapeDtypeStruct((expert_count * 2 * capacity, LANES), BF),
        4 * slots * tokens * feature_width,
        4 * slots * LANES,
        arrays=3,
    )(routes.T, probs.T, grad_rows)
    outgoing = outgoing.reshape(expert_count, 2 * capacity, LANES)
    dense_saved, expert_saved, dense_down, expert_down = after(
        (dense_saved, expert_saved, dense_down, expert_down), outgoing
    )
    received = lax.all_to_all(outgoing, EXPERT, split_axis=0, concat_axis=0, tiled=True)
    received = local_kernel(
        functools.partial(arrange_kernel, capacity),
        jax.ShapeDtypeStruct((feature_width, slots), BF),
        4 * slots * slots * LANES,
        8 * slots * LANES,
    )(after(received.reshape(-1, LANES), grad_half))
    sent_half = gather_columns(received)

    gate_dense, up_dense, sigmoid_dense, dense_units = swiglu_parts(dense_saved[0].T, dense_saved[1].T)
    gate_expert, up_expert, sigmoid_expert, expert_units = swiglu_parts(
        expert_saved[0, 0].T, expert_saved[0, 1].T
    )
    units_other = swap(jnp.concatenate([dense_units, expert_units], axis=1))
    dense_units_other, expert_units_other = units_other[:, :tokens], units_other[:, tokens:]
    split = local_kernel(
        functools.partial(split_kernel, runs),
        [jax.ShapeDtypeStruct((hidden_count, model_width // 2), BF)] * 2,
        0,
        4 * hidden_count * model_width,
        1,
        1,
    )
    dense_mine, dense_theirs = split(half_index, dense_down)
    dense_theirs = swap(dense_theirs)
    expert_mine, expert_theirs = split(half_index, after(expert_down[0], dense_mine))

    first = half == 0
    units = (jnp.where(first, dense_units, dense_units_other), jnp.where(first, dense_units_other, dense_units))
    units = after(units, (dense_theirs, expert_theirs))
    terms = scatter_terms(grad_half, units)
    expert_theirs = swap(after(expert_theirs, terms))
    came = lax.all_to_all(terms, EXPERT, split_axis=0, concat_axis=0, tiled=True)
    grad_half = after(grad_half, terms)
    cot_other = jnp.einsum("hf,fr->hr", dense_theirs, grad_half, preferred_element_type=F32)
    cot_own = jnp.einsum("hf,fr->hr", dense_mine, grad_half, preferred_element_type=F32)
    dense_cot = cot_own + swap(cot_other.astype(BF)).astype(F32)

    dense_pre_grad = pre_cotangents(dense_cot, gate_dense, up_dense, sigmoid_dense).transpose(0, 2, 1)
    sent_half = after(sent_half, dense_pre_grad)

    cot_other = jnp.einsum("hf,fr->hr", expert_theirs, sent_half, preferred_element_type=F32)
    cot_other = cot_other.astype(BF)
    sent_half = after(sent_half, cot_other)
    cot_other = swap(cot_other)
    grad_other = jnp.einsum("hr,fr->hf", expert_units_other, sent_half, preferred_element_type=F32)
    grad_other = grad_other.astype(BF)
    sent_half, came = after((sent_half, came), grad_other)
    grad_other = swap(grad_other)
    dense_share = scatter_total(came, model_width // expert_count, hidden_count)
    grad_own = jnp.einsum("hr,fr->hf", expert_units, sent_half, preferred_element_type=F32).astype(BF)
    cot_own = jnp.einsum("hf,fr->hr", expert_mine, sent_half, preferred_element_type=F32)
    expert_cot = cot_own + cot_other.astype(F32)
    expert_down_grad = local_kernel(
        functools.partial(join_kernel, runs),
        jax.ShapeDtypeStruct((hidden_count, model_width), BF),
        0,
        4 * hidden_count * model_width,
        1,
        2,
    )(half_index, grad_own, grad_other)[None]

    expert_pre_grad = pre_cotangents(expert_cot, gate_expert, up_expert, sigmoid_expert)
    expert_pre_grad = expert_pre_grad.transpose(0, 2, 1)[None]
    dense_down_grad = dense_share.T
    return (expert_pre_grad, expert_down_grad, dense_pre_grad, dense_down_grad)


def solution(mesh):
    experts, tensors, pairs = mesh.devices.shape
    chips = min(8, experts // 2)
    fine = Mesh(
        mesh.devices.reshape(experts // (2 * chips), chips, 2, tensors, pairs),
        EXPERT + SHARE,
    )
    return jax.shard_map(
        body,
        mesh=fine,
        in_specs=(
            P(EXPERT, SHARE),
            P(EXPERT, None),
            P(EXPERT, None),
            P(EXPERT, SHARE, None),
            P(EXPERT, None, None, SHARE),
            P(SHARE, None),
            P(None, EXPERT, SHARE),
        ),
        out_specs=(
            P(EXPERT, None, None, SHARE),
            P(EXPERT, SHARE, None),
            P(None, EXPERT, SHARE),
            P(SHARE, EXPERT),
        ),
        check_vma=False,
    )
```

```python
import functools

import jax
import jax.numpy as jnp
from jax import lax
from jax.experimental import pallas as pl
from jax.experimental.pallas import tpu as pltpu
from jax.sharding import Mesh, PartitionSpec as P

BF = jnp.bfloat16
F32 = jnp.float32
EXPERT = ("zh", "x", "core")
SHARE = ("y", "zl")
LANES = 128
STACK = 16
VMEM_LIMIT = 48 * 1024 * 1024


def local_kernel(kernel, outs, flops, moved, scalars=0, arrays=1):
    specs = [pl.BlockSpec(memory_space=pltpu.SMEM)] * scalars
    return pl.pallas_call(
        kernel,
        out_shape=outs,
        in_specs=specs + [pl.BlockSpec(memory_space=pltpu.VMEM)] * arrays,
        compiler_params=pltpu.CompilerParams(vmem_limit_bytes=VMEM_LIMIT),
        cost_estimate=pl.CostEstimate(flops=flops, bytes_accessed=moved, transcendentals=0),
    )


def dispatch_kernel(experts, capacity, routes_ref, probs_ref, grad_ref, out_ref):
    tokens, features = routes_ref.shape[1], grad_ref.shape[0]
    rows = out_ref.shape[0]
    first, second = routes_ref[0:1, :], routes_ref[1:2, :]
    names = lax.broadcasted_iota(jnp.int32, (experts, tokens), 0)
    on_first, on_second = names == first, names == second
    named = (on_first | on_second).astype(F32).astype(BF)
    earlier = lax.broadcasted_iota(jnp.int32, (tokens, tokens), 0) < lax.broadcasted_iota(
        jnp.int32, (tokens, tokens), 1
    )
    before = jnp.dot(named, earlier.astype(F32).astype(BF), preferred_element_type=F32)
    place_first = jnp.sum(jnp.where(on_first, before, 0.0), axis=0, keepdims=True)
    place_second = jnp.sum(jnp.where(on_second, before, 0.0), axis=0, keepdims=True)
    slot_first = first * capacity + place_first.astype(jnp.int32)
    slot_second = second * capacity + place_second.astype(jnp.int32)
    step = rows // 4
    for part in range(4):
        row = lax.broadcasted_iota(jnp.int32, (step, 1), 0) + part * step
        slot = row // (2 * capacity) * capacity + row % capacity
        is_first, is_second = slot == slot_first, slot == slot_second
        table = jnp.where(is_first, probs_ref[0:1, :], jnp.where(is_second, probs_ref[1:2, :], 0.0))
        weight = jnp.sum(table, axis=1, keepdims=True)
        onehot = (is_first | is_second).astype(F32).astype(BF)
        picked = lax.dot_general(
            onehot, grad_ref[...], (((1,), (1,)), ((), ())), preferred_element_type=F32
        )
        sent = picked * weight
        low = sent[:, :LANES]
        high = jnp.concatenate(
            [sent[:, LANES:], jnp.zeros((step, 2 * LANES - features), F32)], axis=1
        )
        out_ref[part * step : (part + 1) * step, :] = jnp.where(
            row % (2 * capacity) < capacity, low, high
        ).astype(BF)


def arrange_kernel(capacity, came_ref, out_ref):
    rows, features, slots = came_ref.shape[0], out_ref.shape[0], out_ref.shape[1]
    parts = 2
    row_step, slot_step = rows // parts, slots // parts
    row = lax.broadcasted_iota(jnp.int32, (row_step, 1), 0)
    slot = lax.broadcasted_iota(jnp.int32, (1, slot_step), 1)
    wanted = slot // capacity * (2 * capacity) + slot % capacity
    for half in range(2):
        pick = (row == wanted + half * capacity).astype(F32).astype(BF)
        for part in range(parts):
            block = came_ref[part * row_step : (part + 1) * row_step, :]
            value = lax.dot_general(
                block, pick, (((0,), (0,)), ((), ())), preferred_element_type=F32
            ).astype(BF)
            top = min(features - half * LANES, LANES)
            out_ref[half * LANES : half * LANES + top, part * slot_step : (part + 1) * slot_step] = value[
                :top, :
            ]


def split_kernel(runs, half_ref, weights_ref, mine_ref, theirs_ref):
    width = weights_ref.shape[1] // (2 * runs)

    def columns(half):
        return jnp.concatenate(
            [weights_ref[:, (2 * run + half) * width : (2 * run + half + 1) * width] for run in range(runs)],
            axis=1,
        )

    for half in range(2):

        @pl.when(half_ref[0] == half)
        def _():
            mine_ref[...] = columns(half)
            theirs_ref[...] = columns(1 - half)


def join_kernel(runs, half_ref, own_ref, other_ref, out_ref):
    width = own_ref.shape[1] // runs

    def joined(low_ref, high_ref):
        pieces = []
        for run in range(runs):
            for ref in (low_ref, high_ref):
                pieces.append(ref[:, run * width : (run + 1) * width])
        return jnp.concatenate(pieces, axis=1)

    @pl.when(half_ref[0] == 0)
    def _():
        out_ref[...] = joined(own_ref, other_ref)

    @pl.when(half_ref[0] == 1)
    def _():
        out_ref[...] = joined(other_ref, own_ref)


def swiglu_parts(gate_saved, up_saved):
    gate_pre = gate_saved.astype(F32)
    up_pre = up_saved.astype(F32)
    sigmoid_gate = jax.nn.sigmoid(gate_pre)
    hidden = (gate_pre * sigmoid_gate * up_pre).astype(BF)
    return (gate_pre, up_pre, sigmoid_gate, hidden)


def pre_cotangents(hidden_cot, gate_pre, up_pre, sigmoid_gate):
    gate_cot = hidden_cot * up_pre * sigmoid_gate * (1.0 + gate_pre * (1.0 - sigmoid_gate))
    up_cot = hidden_cot * gate_pre * sigmoid_gate
    return jnp.stack([gate_cot, up_cot]).astype(BF)


def after(values, earlier):
    return lax.optimization_barrier((values, earlier))[0]


def swap(values):
    return lax.ppermute(values, "zl", [(0, 1), (1, 0)])


def gather_columns(rows):
    whole = lax.all_gather(rows, "y", axis=0, tiled=False)
    return whole.reshape(-1, rows.shape[1])


def terms_kernel(runs, grad_ref, first_ref, second_ref, out_ref):
    parts, rows, _ = out_ref.shape
    hidden, width = first_ref.shape[0], rows - STACK
    span, step = parts // (2 * runs), grad_ref.shape[0] // runs
    stack, extra = rows - width, hidden - LANES
    for run in range(runs):
        grads = grad_ref[run * step : run * step + span * width, :]
        for half, ref in enumerate((first_ref, second_ref)):
            value = lax.dot_general(
                grads, ref[...], (((1,), (1,)), ((), ())), preferred_element_type=F32
            )
            for index in range(span):
                block = value[index * width : (index + 1) * width, :]
                last = jnp.concatenate(
                    [block[:, LANES:], jnp.zeros((-width % stack, extra), F32)], axis=0
                )
                count = last.shape[0] // stack
                last = jnp.concatenate(
                    [last[piece * stack : (piece + 1) * stack, :] for piece in range(count)]
                    + [jnp.zeros((stack, LANES - count * extra), F32)],
                    axis=1,
                )
                out_ref[(run * 2 + half) * span + index] = jnp.concatenate(
                    [block[:, :LANES], last], axis=0
                ).astype(BF)


def total_kernel(came_ref, out_ref):
    parts, rows, _ = came_ref.shape
    width, hidden = out_ref.shape
    stack, extra = rows - width, hidden - LANES
    total = came_ref[0].astype(F32)
    for part in range(1, parts):
        total = total + came_ref[part].astype(F32)
    last = jnp.concatenate(
        [total[width:, piece * extra : (piece + 1) * extra] for piece in range(-(-width // stack))], axis=0
    )
    out_ref[...] = jnp.concatenate([total[:width, :], last[:width, :]], axis=1).astype(BF)


def scatter_terms(grad_runs, units, width):
    parts, runs = lax.axis_size(EXPERT), lax.axis_size("y")
    return local_kernel(
        functools.partial(terms_kernel, runs),
        jax.ShapeDtypeStruct((parts, width + STACK, LANES), BF),
        2 * parts * width * units[0].size,
        4 * parts * width * LANES,
        0,
        3,
    )(grad_runs, *units)


def scatter_total(came, width, hidden):
    mine = local_kernel(
        total_kernel, jax.ShapeDtypeStruct((width, hidden), BF), came.size, 2 * came.size
    )(came)
    chips = lax.axis_size("x")
    route = [(2 * x + z, 2 * (x ^ 2) + (1 - z)) for x in range(chips) for z in range(2)]
    other = lax.ppermute(mine, ("x", "zl"), route)
    here = lax.axis_index("x") // 2 % 2 == lax.axis_index("zl")
    return jnp.where(here, mine, other)


def body(grad_out, routes, probs, expert_down, expert_saved, dense_down, dense_saved):
    expert_count, runs = lax.axis_size(EXPERT), lax.axis_size("y")
    slots, hidden_count = expert_saved.shape[2:]
    capacity = slots // expert_count
    tokens, feature_width = grad_out.shape
    model_width = dense_down.shape[1]
    half = lax.axis_index("zl").astype(jnp.int32)
    half_index = half.reshape(1)
    grad_rows = grad_out.T

    padded = -feature_width % LANES
    grad_runs = gather_columns(jnp.pad(grad_rows, ((0, padded), (0, 0))))

    outgoing = local_kernel(
        functools.partial(dispatch_kernel, expert_count, capacity),
        jax.ShapeDtypeStruct((expert_count * 2 * capacity, LANES), BF),
        4 * slots * tokens * feature_width,
        4 * slots * LANES,
        arrays=3,
    )(routes.T, probs.T, grad_rows)
    outgoing = outgoing.reshape(expert_count, 2 * capacity, LANES)
    dense_saved, expert_saved, dense_down, expert_down = after(
        (dense_saved, expert_saved, dense_down, expert_down), outgoing
    )
    received = lax.all_to_all(outgoing, EXPERT, split_axis=0, concat_axis=0, tiled=True)
    gate_dense, up_dense, sigmoid_dense, dense_units = swiglu_parts(dense_saved[0].T, dense_saved[1].T)
    gate_expert, up_expert, sigmoid_expert, expert_units = swiglu_parts(
        expert_saved[0, 0].T, expert_saved[0, 1].T
    )
    units_other = swap(jnp.concatenate([dense_units, expert_units], axis=1))
    dense_units_other, expert_units_other = units_other[:, :tokens], units_other[:, tokens:]
    received = local_kernel(
        functools.partial(arrange_kernel, capacity),
        jax.ShapeDtypeStruct((feature_width, slots), BF),
        4 * slots * slots * LANES,
        8 * slots * LANES,
    )(received.reshape(-1, LANES))
    sent_half = gather_columns(received)

    split = local_kernel(
        functools.partial(split_kernel, runs),
        [jax.ShapeDtypeStruct((hidden_count, model_width // 2), BF)] * 2,
        0,
        4 * hidden_count * model_width,
        1,
        1,
    )
    dense_mine, dense_theirs = split(half_index, dense_down)
    dense_swapped = swap(dense_theirs)
    expert_mine, expert_theirs = split(half_index, after(expert_down[0], dense_mine))

    first = half == 0
    units = (jnp.where(first, dense_units, dense_units_other), jnp.where(first, dense_units_other, dense_units))
    units = after(units, (received, dense_theirs, expert_theirs))
    terms = scatter_terms(grad_runs, units, model_width // expert_count)
    expert_theirs = swap(after(expert_theirs, terms))
    dense_theirs = dense_swapped
    came = lax.all_to_all(terms, EXPERT, split_axis=0, concat_axis=0, tiled=True)
    grad_runs = after(grad_runs, terms).reshape(runs, -1, tokens)
    grad_half = grad_runs[:, :feature_width].reshape(-1, tokens)
    dense_other = jnp.einsum("hf,fr->hr", dense_theirs, grad_half, preferred_element_type=F32).astype(BF)
    dense_cot = jnp.einsum("hf,fr->hr", dense_mine, grad_half, preferred_element_type=F32)
    sent_half = after(sent_half, (dense_other, dense_cot))

    grad_other = jnp.einsum("hr,fr->hf", expert_units_other, sent_half, preferred_element_type=F32)
    grad_other = grad_other.astype(BF)
    sent_half = after(sent_half, grad_other)
    grad_other = swap(grad_other)
    cot_other = jnp.einsum("hf,fr->hr", expert_theirs, sent_half, preferred_element_type=F32)
    cot_other = jnp.concatenate([dense_other, cot_other.astype(BF)], axis=1)
    sent_half, came = after((sent_half, came), cot_other)
    cot_other = swap(cot_other)
    dense_share = scatter_total(came, model_width // expert_count, hidden_count)
    grad_own = jnp.einsum("hr,fr->hf", expert_units, sent_half, preferred_element_type=F32).astype(BF)
    cot_own = jnp.einsum("hf,fr->hr", expert_mine, sent_half, preferred_element_type=F32)
    cot_other = cot_other.astype(F32)
    expert_cot = cot_own + cot_other[:, tokens:]
    dense_cot = dense_cot + cot_other[:, :tokens]
    dense_pre_grad = pre_cotangents(dense_cot, gate_dense, up_dense, sigmoid_dense).transpose(0, 2, 1)
    expert_down_grad = local_kernel(
        functools.partial(join_kernel, runs),
        jax.ShapeDtypeStruct((hidden_count, model_width), BF),
        0,
        4 * hidden_count * model_width,
        1,
        2,
    )(half_index, grad_own, grad_other)[None]

    expert_pre_grad = pre_cotangents(expert_cot, gate_expert, up_expert, sigmoid_expert)
    expert_pre_grad = expert_pre_grad.transpose(0, 2, 1)[None]
    dense_down_grad = dense_share.T
    return (expert_pre_grad, expert_down_grad, dense_pre_grad, dense_down_grad)


def solution(mesh):
    experts, tensors, pairs = mesh.devices.shape
    chips = min(8, experts // 2)
    fine = Mesh(
        mesh.devices.reshape(experts // (2 * chips), chips, 2, tensors, pairs),
        EXPERT + SHARE,
    )
    return jax.shard_map(
        body,
        mesh=fine,
        in_specs=(
            P(EXPERT, SHARE),
            P(EXPERT, None),
            P(EXPERT, None),
            P(EXPERT, SHARE, None),
            P(EXPERT, None, None, SHARE),
            P(SHARE, None),
            P(None, EXPERT, SHARE),
        ),
        out_specs=(
            P(EXPERT, None, None, SHARE),
            P(EXPERT, SHARE, None),
            P(None, EXPERT, SHARE),
            P(SHARE, EXPERT),
        ),
        check_vma=False,
    )
```

```python
import functools

import jax
import jax.numpy as jnp
from jax import lax
from jax.experimental import pallas as pl
from jax.experimental.pallas import tpu as pltpu
from jax.sharding import Mesh, PartitionSpec as P

BF = jnp.bfloat16
F32 = jnp.float32
EXPERT = ("zh", "x", "core")
SHARE = ("y", "zl")
LANES = 128
STACK = 16
VMEM_LIMIT = 48 * 1024 * 1024


def local_kernel(kernel, outs, flops, moved, scalars=0, arrays=1):
    specs = [pl.BlockSpec(memory_space=pltpu.SMEM)] * scalars
    return pl.pallas_call(
        kernel,
        out_shape=outs,
        in_specs=specs + [pl.BlockSpec(memory_space=pltpu.VMEM)] * arrays,
        compiler_params=pltpu.CompilerParams(vmem_limit_bytes=VMEM_LIMIT),
        cost_estimate=pl.CostEstimate(flops=flops, bytes_accessed=moved, transcendentals=0),
    )


def dispatch_kernel(experts, capacity, routes_ref, probs_ref, grad_ref, out_ref):
    tokens, features = routes_ref.shape[1], grad_ref.shape[0]
    rows = out_ref.shape[0]
    first, second = routes_ref[0:1, :], routes_ref[1:2, :]
    names = lax.broadcasted_iota(jnp.int32, (experts, tokens), 0)
    on_first, on_second = names == first, names == second
    named = (on_first | on_second).astype(F32).astype(BF)
    earlier = lax.broadcasted_iota(jnp.int32, (tokens, tokens), 0) < lax.broadcasted_iota(
        jnp.int32, (tokens, tokens), 1
    )
    before = jnp.dot(named, earlier.astype(F32).astype(BF), preferred_element_type=F32)
    place_first = jnp.sum(jnp.where(on_first, before, 0.0), axis=0, keepdims=True)
    place_second = jnp.sum(jnp.where(on_second, before, 0.0), axis=0, keepdims=True)
    slot_first = first * capacity + place_first.astype(jnp.int32)
    slot_second = second * capacity + place_second.astype(jnp.int32)
    step = rows // 4
    for part in range(4):
        row = lax.broadcasted_iota(jnp.int32, (step, 1), 0) + part * step
        slot = row // (2 * capacity) * capacity + row % capacity
        is_first, is_second = slot == slot_first, slot == slot_second
        table = jnp.where(is_first, probs_ref[0:1, :], jnp.where(is_second, probs_ref[1:2, :], 0.0))
        weight = jnp.sum(table, axis=1, keepdims=True)
        onehot = (is_first | is_second).astype(F32).astype(BF)
        picked = lax.dot_general(
            onehot, grad_ref[...], (((1,), (1,)), ((), ())), preferred_element_type=F32
        )
        sent = picked * weight
        low = sent[:, :LANES]
        high = jnp.concatenate(
            [sent[:, LANES:], jnp.zeros((step, 2 * LANES - features), F32)], axis=1
        )
        out_ref[part * step : (part + 1) * step, :] = jnp.where(
            row % (2 * capacity) < capacity, low, high
        ).astype(BF)


def arrange_kernel(capacity, came_ref, out_ref):
    rows, features, slots = came_ref.shape[0], out_ref.shape[0], out_ref.shape[1]
    parts = 2
    row_step, slot_step = rows // parts, slots // parts
    row = lax.broadcasted_iota(jnp.int32, (row_step, 1), 0)
    slot = lax.broadcasted_iota(jnp.int32, (1, slot_step), 1)
    wanted = slot // capacity * (2 * capacity) + slot % capacity
    for half in range(2):
        pick = (row == wanted + half * capacity).astype(F32).astype(BF)
        for part in range(parts):
            block = came_ref[part * row_step : (part + 1) * row_step, :]
            value = lax.dot_general(
                block, pick, (((0,), (0,)), ((), ())), preferred_element_type=F32
            ).astype(BF)
            top = min(features - half * LANES, LANES)
            out_ref[half * LANES : half * LANES + top, part * slot_step : (part + 1) * slot_step] = value[
                :top, :
            ]


def split_kernel(runs, half_ref, weights_ref, mine_ref, theirs_ref):
    width = weights_ref.shape[1] // (2 * runs)

    def columns(half):
        return jnp.concatenate(
            [weights_ref[:, (2 * run + half) * width : (2 * run + half + 1) * width] for run in range(runs)],
            axis=1,
        )

    for half in range(2):

        @pl.when(half_ref[0] == half)
        def _():
            mine_ref[...] = columns(half)
            theirs_ref[...] = columns(1 - half)


def join_kernel(runs, half_ref, own_ref, other_ref, out_ref):
    width = own_ref.shape[1] // runs

    def joined(low_ref, high_ref):
        pieces = []
        for run in range(runs):
            for ref in (low_ref, high_ref):
                pieces.append(ref[:, run * width : (run + 1) * width])
        return jnp.concatenate(pieces, axis=1)

    @pl.when(half_ref[0] == 0)
    def _():
        out_ref[...] = joined(own_ref, other_ref)

    @pl.when(half_ref[0] == 1)
    def _():
        out_ref[...] = joined(other_ref, own_ref)


def swiglu_parts(gate_saved, up_saved):
    gate_pre = gate_saved.astype(F32)
    up_pre = up_saved.astype(F32)
    sigmoid_gate = jax.nn.sigmoid(gate_pre)
    hidden = (gate_pre * sigmoid_gate * up_pre).astype(BF)
    return (gate_pre, up_pre, sigmoid_gate, hidden)


def pre_cotangents(hidden_cot, gate_pre, up_pre, sigmoid_gate):
    gate_cot = hidden_cot * up_pre * sigmoid_gate * (1.0 + gate_pre * (1.0 - sigmoid_gate))
    up_cot = hidden_cot * gate_pre * sigmoid_gate
    return jnp.stack([gate_cot, up_cot]).astype(BF)


def after(values, earlier):
    return lax.optimization_barrier((values, earlier))[0]


def swap(values):
    return lax.ppermute(values, "zl", [(0, 1), (1, 0)])


def gather_columns(rows):
    whole = lax.all_gather(rows, "y", axis=0, tiled=False)
    return whole.reshape(-1, rows.shape[1])


def terms_kernel(runs, core_ref, grad_ref, first_ref, second_ref, mine_ref, theirs_ref):
    pairs, rows, _ = mine_ref.shape
    hidden, width = first_ref.shape[0], rows - STACK
    span = pairs // runs
    extra, missing = hidden - LANES, -width % STACK
    for core in range(2):

        @pl.when(core_ref[0] == core)
        def _():
            for run in range(runs):
                grads = grad_ref[run * span * width : (run + 1) * span * width, :]
                for half, ref in enumerate((first_ref, second_ref)):
                    value = lax.dot_general(
                        grads, ref[...], (((1,), (1,)), ((), ())), preferred_element_type=F32
                    )
                    for index in range(span):
                        block = value[index * width : (index + 1) * width, :]
                        last = jnp.concatenate([block[:, LANES:], jnp.zeros((missing, extra), F32)], axis=0)
                        count = last.shape[0] // STACK
                        last = jnp.concatenate(
                            [last[piece * STACK : (piece + 1) * STACK, :] for piece in range(count)]
                            + [jnp.zeros((STACK, LANES - count * extra), F32)],
                            axis=1,
                        )
                        block = jnp.concatenate([block[:, :LANES], last], axis=0)
                        place = (run * 2 + half) * span + index
                        if place % 2 == core:
                            mine_ref[place // 2] = block
                        else:
                            theirs_ref[place // 2] = block.astype(BF)


def pair_kernel(mine_ref, other_ref, out_ref):
    out_ref[...] = (mine_ref[...] + other_ref[...].astype(F32)).astype(BF)


def total_kernel(came_ref, out_ref):
    parts, rows, _ = came_ref.shape
    width, hidden = out_ref.shape
    stack, extra = rows - width, hidden - LANES
    total = came_ref[0].astype(F32)
    for part in range(1, parts):
        total = total + came_ref[part].astype(F32)
    last = jnp.concatenate(
        [total[width:, piece * extra : (piece + 1) * extra] for piece in range(-(-width // stack))], axis=0
    )
    out_ref[...] = jnp.concatenate([total[:width, :], last[:width, :]], axis=1).astype(BF)


def scatter_total(came, width, hidden):
    mine = local_kernel(
        total_kernel, jax.ShapeDtypeStruct((width, hidden), BF), came.size, 2 * came.size
    )(came)
    chips = lax.axis_size("x")
    route = [(2 * x + z, 2 * (x ^ 2) + (1 - z)) for x in range(chips) for z in range(2)]
    other = lax.ppermute(mine, ("x", "zl"), route)
    here = lax.axis_index("x") // 2 % 2 == lax.axis_index("zl")
    return jnp.where(here, mine, other)


def body(grad_out, routes, probs, expert_down, expert_saved, dense_down, dense_saved):
    expert_count, runs = lax.axis_size(EXPERT), lax.axis_size("y")
    slots, hidden_count = expert_saved.shape[2:]
    capacity = slots // expert_count
    tokens, feature_width = grad_out.shape
    model_width = dense_down.shape[1]
    width = model_width // expert_count
    half = lax.axis_index("zl").astype(jnp.int32)
    half_index = half.reshape(1)
    core_index = lax.axis_index("core").astype(jnp.int32).reshape(1)
    first = half == 0
    grad_rows = grad_out.T

    outgoing = local_kernel(
        functools.partial(dispatch_kernel, expert_count, capacity),
        jax.ShapeDtypeStruct((expert_count * 2 * capacity, LANES), BF),
        4 * slots * tokens * feature_width,
        4 * slots * LANES,
        0,
        3,
    )(routes.T, probs.T, grad_rows)
    outgoing = outgoing.reshape(expert_count, 2 * capacity, LANES)
    received = lax.all_to_all(outgoing, EXPERT, split_axis=0, concat_axis=0, tiled=True)

    dense_saved = after(dense_saved, outgoing)
    gate_dense, up_dense, sigmoid_dense, dense_units = swiglu_parts(dense_saved[0].T, dense_saved[1].T)
    dense_units_other = swap(dense_units)
    grad_half = gather_columns(after(grad_rows, (outgoing, dense_units)))

    received = local_kernel(
        functools.partial(arrange_kernel, capacity),
        jax.ShapeDtypeStruct((feature_width, slots), BF),
        4 * slots * slots * LANES,
        8 * slots * LANES,
    )(after(received.reshape(-1, LANES), (grad_half, dense_units_other)))
    sent_half = gather_columns(received)

    units = (jnp.where(first, dense_units, dense_units_other), jnp.where(first, dense_units_other, dense_units))
    block = (expert_count // 2, width + STACK, LANES)
    mine, theirs = local_kernel(
        functools.partial(terms_kernel, runs),
        [jax.ShapeDtypeStruct(block, F32), jax.ShapeDtypeStruct(block, BF)],
        2 * model_width * hidden_count * tokens,
        8 * model_width * LANES,
        1,
        3,
    )(core_index, grad_half, *after(units, received))
    expert_saved, dense_down, expert_down = after((expert_saved, dense_down, expert_down), theirs)
    other = lax.ppermute(theirs, "core", [(0, 1), (1, 0)])

    gate_expert, up_expert, sigmoid_expert, expert_units = swiglu_parts(
        expert_saved[0, 0].T, expert_saved[0, 1].T
    )
    split = local_kernel(
        functools.partial(split_kernel, runs),
        [jax.ShapeDtypeStruct((hidden_count, model_width // 2), BF)] * 2,
        0,
        4 * hidden_count * model_width,
        1,
        1,
    )
    dense_mine, dense_theirs = split(half_index, dense_down)
    dense_theirs = swap(dense_theirs)
    expert_mine, expert_theirs = split(half_index, after(expert_down[0], dense_mine))

    pairs = local_kernel(
        pair_kernel, jax.ShapeDtypeStruct(block, BF), mine.size, 8 * mine.size, 0, 2
    )(mine, after(other, (dense_theirs, expert_units, expert_theirs)))
    came = lax.all_to_all(pairs, ("zh", "x"), split_axis=0, concat_axis=0, tiled=True)
    expert_theirs, expert_units_other = after((expert_theirs, expert_units), theirs)
    expert_units_other = swap(expert_units_other)
    expert_theirs = swap(expert_theirs)

    grad_half = after(grad_half, pairs)
    dense_other = jnp.einsum("hf,fr->hr", dense_theirs, grad_half, preferred_element_type=F32)
    dense_cot = jnp.einsum("hf,fr->hr", dense_mine, grad_half, preferred_element_type=F32)
    dense_cot = dense_cot + swap(dense_other.astype(BF)).astype(F32)
    dense_pre_grad = pre_cotangents(dense_cot, gate_dense, up_dense, sigmoid_dense).transpose(0, 2, 1)
    dense_share = scatter_total(came, width, hidden_count)
    sent_half = after(sent_half, (dense_pre_grad, dense_share))

    cot_other = jnp.einsum("hf,fr->hr", expert_theirs, sent_half, preferred_element_type=F32)
    cot_other = cot_other.astype(BF)
    sent_half = after(sent_half, cot_other)
    cot_other = swap(cot_other)
    grad_other = jnp.einsum("hr,fr->hf", expert_units_other, sent_half, preferred_element_type=F32)
    grad_other = grad_other.astype(BF)
    sent_half = after(sent_half, grad_other)
    grad_other = swap(grad_other)
    grad_own = jnp.einsum("hr,fr->hf", expert_units, sent_half, preferred_element_type=F32).astype(BF)
    cot_own = jnp.einsum("hf,fr->hr", expert_mine, sent_half, preferred_element_type=F32)
    expert_cot = cot_own + cot_other.astype(F32)
    expert_pre_grad = pre_cotangents(expert_cot, gate_expert, up_expert, sigmoid_expert)
    expert_down_grad = local_kernel(
        functools.partial(join_kernel, runs),
        jax.ShapeDtypeStruct((hidden_count, model_width), BF),
        0,
        4 * hidden_count * model_width,
        1,
        2,
    )(half_index, grad_own, grad_other)[None]
    expert_pre_grad = expert_pre_grad.transpose(0, 2, 1)[None]
    return (expert_pre_grad, expert_down_grad, dense_pre_grad, dense_share.T)


def solution(mesh):
    experts, tensors, pairs = mesh.devices.shape
    chips = min(8, experts // 2)
    fine = Mesh(
        mesh.devices.reshape(experts // (2 * chips), chips, 2, tensors, pairs),
        EXPERT + SHARE,
    )
    return jax.shard_map(
        body,
        mesh=fine,
        in_specs=(
            P(EXPERT, SHARE),
            P(EXPERT, None),
            P(EXPERT, None),
            P(EXPERT, SHARE, None),
            P(EXPERT, None, None, SHARE),
            P(SHARE, None),
            P(None, EXPERT, SHARE),
        ),
        out_specs=(
            P(EXPERT, None, None, SHARE),
            P(EXPERT, SHARE, None),
            P(None, EXPERT, SHARE),
            P(SHARE, EXPERT),
        ),
        check_vma=False,
    )
```

```python
import functools

import jax
import jax.numpy as jnp
from jax import lax
from jax.experimental import pallas as pl
from jax.experimental.pallas import tpu as pltpu
from jax.sharding import Mesh, PartitionSpec as P

BF = jnp.bfloat16
F32 = jnp.float32
EXPERT = ("zh", "x", "core")
SHARE = ("y", "zl")
LANES = 128
STACK = 16
VMEM_LIMIT = 48 * 1024 * 1024


def local_kernel(kernel, outs, flops, moved, scalars=0, arrays=1):
    specs = [pl.BlockSpec(memory_space=pltpu.SMEM)] * scalars
    return pl.pallas_call(
        kernel,
        out_shape=outs,
        in_specs=specs + [pl.BlockSpec(memory_space=pltpu.VMEM)] * arrays,
        compiler_params=pltpu.CompilerParams(vmem_limit_bytes=VMEM_LIMIT),
        cost_estimate=pl.CostEstimate(flops=flops, bytes_accessed=moved, transcendentals=0),
    )


def dispatch_kernel(experts, capacity, routes_in, probs_in, grad_in, out_ref, routes_ref, probs_ref, grad_ref, sems):
    copies = [
        pltpu.make_async_copy(routes_in, routes_ref, sems.at[0]),
        pltpu.make_async_copy(probs_in, probs_ref, sems.at[1]),
        pltpu.make_async_copy(grad_in, grad_ref, sems.at[2]),
    ]
    for copy in copies:
        copy.start()
    for copy in copies:
        copy.wait()
    tokens, features = routes_ref.shape[1], grad_ref.shape[0]
    rows = out_ref.shape[0]
    first, second = routes_ref[0:1, :], routes_ref[1:2, :]
    names = lax.broadcasted_iota(jnp.int32, (experts, tokens), 0)
    on_first, on_second = names == first, names == second
    named = (on_first | on_second).astype(F32).astype(BF)
    earlier = lax.broadcasted_iota(jnp.int32, (tokens, tokens), 0) < lax.broadcasted_iota(
        jnp.int32, (tokens, tokens), 1
    )
    before = jnp.dot(named, earlier.astype(F32).astype(BF), preferred_element_type=F32)
    place_first = jnp.sum(jnp.where(on_first, before, 0.0), axis=0, keepdims=True)
    place_second = jnp.sum(jnp.where(on_second, before, 0.0), axis=0, keepdims=True)
    slot_first = first * capacity + place_first.astype(jnp.int32)
    slot_second = second * capacity + place_second.astype(jnp.int32)
    step = rows // 4
    for part in range(4):
        row = lax.broadcasted_iota(jnp.int32, (step, 1), 0) + part * step
        slot = row // (2 * capacity) * capacity + row % capacity
        is_first, is_second = slot == slot_first, slot == slot_second
        table = jnp.where(is_first, probs_ref[0:1, :], jnp.where(is_second, probs_ref[1:2, :], 0.0))
        weight = jnp.sum(table, axis=1, keepdims=True)
        onehot = (is_first | is_second).astype(F32).astype(BF)
        picked = lax.dot_general(
            onehot, grad_ref[...], (((1,), (1,)), ((), ())), preferred_element_type=F32
        )
        sent = picked * weight
        low = sent[:, :LANES]
        high = jnp.concatenate(
            [sent[:, LANES:], jnp.zeros((step, 2 * LANES - features), F32)], axis=1
        )
        out_ref[part * step : (part + 1) * step, :] = jnp.where(
            row % (2 * capacity) < capacity, low, high
        ).astype(BF)


def arrange_kernel(capacity, came_ref, out_ref):
    rows, features, slots = came_ref.shape[0], out_ref.shape[0], out_ref.shape[1]
    parts = 2
    row_step, slot_step = rows // parts, slots // parts
    row = lax.broadcasted_iota(jnp.int32, (row_step, 1), 0)
    slot = lax.broadcasted_iota(jnp.int32, (1, slot_step), 1)
    wanted = slot // capacity * (2 * capacity) + slot % capacity
    for half in range(2):
        pick = (row == wanted + half * capacity).astype(F32).astype(BF)
        for part in range(parts):
            block = came_ref[part * row_step : (part + 1) * row_step, :]
            value = lax.dot_general(
                block, pick, (((0,), (0,)), ((), ())), preferred_element_type=F32
            ).astype(BF)
            top = min(features - half * LANES, LANES)
            out_ref[half * LANES : half * LANES + top, part * slot_step : (part + 1) * slot_step] = value[
                :top, :
            ]


def split_kernel(runs, half_ref, weights_ref, mine_ref, theirs_ref):
    width = weights_ref.shape[1] // (2 * runs)

    def columns(half):
        return jnp.concatenate(
            [weights_ref[:, (2 * run + half) * width : (2 * run + half + 1) * width] for run in range(runs)],
            axis=1,
        )

    for half in range(2):

        @pl.when(half_ref[0] == half)
        def _():
            mine_ref[...] = columns(half)
            theirs_ref[...] = columns(1 - half)


def swiglu_parts(gate_saved, up_saved):
    gate_pre = gate_saved.astype(F32)
    up_pre = up_saved.astype(F32)
    sigmoid_gate = jax.nn.sigmoid(gate_pre)
    hidden = (gate_pre * sigmoid_gate * up_pre).astype(BF)
    return (gate_pre, up_pre, sigmoid_gate, hidden)


def pre_cotangents(hidden_cot, gate_pre, up_pre, sigmoid_gate):
    gate_cot = hidden_cot * up_pre * sigmoid_gate * (1.0 + gate_pre * (1.0 - sigmoid_gate))
    up_cot = hidden_cot * gate_pre * sigmoid_gate
    return jnp.stack([gate_cot, up_cot]).astype(BF)


def after(values, earlier):
    return lax.optimization_barrier((values, earlier))[0]


def swap(values):
    return lax.ppermute(values, "zl", [(0, 1), (1, 0)])


def in_order(own, other, axis):
    first = lax.axis_index("zl") == 0
    return jnp.stack([jnp.where(first, own, other), jnp.where(first, other, own)], axis=axis)


def gather_columns(rows):
    whole = lax.all_gather(rows, "y", axis=0, tiled=False)
    return whole.reshape(-1, rows.shape[1])


def terms_kernel(runs, core_ref, grad_ref, first_ref, second_ref, mine_ref, theirs_ref):
    pairs, rows, _ = mine_ref.shape
    hidden, width = first_ref.shape[0], rows - STACK
    span = pairs // runs
    extra, missing = hidden - LANES, -width % STACK
    for core in range(2):

        @pl.when(core_ref[0] == core)
        def _():
            for run in range(runs):
                grads = grad_ref[run * span * width : (run + 1) * span * width, :]
                for half, ref in enumerate((first_ref, second_ref)):
                    value = lax.dot_general(
                        grads, ref[...], (((1,), (1,)), ((), ())), preferred_element_type=F32
                    )
                    for index in range(span):
                        block = value[index * width : (index + 1) * width, :]
                        last = jnp.concatenate([block[:, LANES:], jnp.zeros((missing, extra), F32)], axis=0)
                        count = last.shape[0] // STACK
                        last = jnp.concatenate(
                            [last[piece * STACK : (piece + 1) * STACK, :] for piece in range(count)]
                            + [jnp.zeros((STACK, LANES - count * extra), F32)],
                            axis=1,
                        )
                        block = jnp.concatenate([block[:, :LANES], last], axis=0)
                        place = (run * 2 + half) * span + index
                        if place % 2 == core:
                            mine_ref[place // 2] = block
                        else:
                            theirs_ref[place // 2] = block.astype(BF)


def pair_kernel(mine_ref, other_ref, out_ref):
    out_ref[...] = (mine_ref[...] + other_ref[...].astype(F32)).astype(BF)


def total_kernel(came_ref, out_ref):
    parts, rows, _ = came_ref.shape
    width, hidden = out_ref.shape
    stack, extra = rows - width, hidden - LANES
    total = came_ref[0].astype(F32)
    for part in range(1, parts):
        total = total + came_ref[part].astype(F32)
    last = jnp.concatenate(
        [total[width:, piece * extra : (piece + 1) * extra] for piece in range(-(-width // stack))], axis=0
    )
    out_ref[...] = jnp.concatenate([total[:width, :], last[:width, :]], axis=1).astype(BF)


def scatter_total(came, width, hidden):
    mine = local_kernel(
        total_kernel, jax.ShapeDtypeStruct((width, hidden), BF), came.size, 2 * came.size
    )(came)
    chips = lax.axis_size("x")
    route = [(2 * x + z, 2 * (x ^ 2) + (1 - z)) for x in range(chips) for z in range(2)]
    other = lax.ppermute(mine, ("x", "zl"), route)
    here = lax.axis_index("x") // 2 % 2 == lax.axis_index("zl")
    return jnp.where(here, mine, other)


def body(grad_out, routes, probs, expert_down, expert_saved, dense_down, dense_saved):
    expert_count, runs = lax.axis_size(EXPERT), lax.axis_size("y")
    slots, hidden_count = expert_saved.shape[2:]
    capacity = slots // expert_count
    tokens, feature_width = grad_out.shape
    model_width = dense_down.shape[1]
    width = model_width // expert_count
    half = lax.axis_index("zl").astype(jnp.int32)
    half_index = half.reshape(1)
    core_index = lax.axis_index("core").astype(jnp.int32).reshape(1)
    first = half == 0
    grad_rows = grad_out.T

    outgoing = pl.pallas_call(
        functools.partial(dispatch_kernel, expert_count, capacity),
        out_shape=jax.ShapeDtypeStruct((expert_count * 2 * capacity, LANES), BF),
        in_specs=[pl.BlockSpec(memory_space=pl.ANY)] * 3,
        scratch_shapes=[
            pltpu.VMEM((2, tokens), jnp.int32),
            pltpu.VMEM((2, tokens), F32),
            pltpu.VMEM((feature_width, tokens), BF),
            pltpu.SemaphoreType.DMA((3,)),
        ],
        compiler_params=pltpu.CompilerParams(vmem_limit_bytes=VMEM_LIMIT),
        cost_estimate=pl.CostEstimate(
            flops=4 * slots * tokens * feature_width, bytes_accessed=4 * slots * LANES, transcendentals=0
        ),
    )(routes.T, probs.T, grad_rows)
    outgoing = outgoing.reshape(expert_count, 2 * capacity, LANES)
    received = lax.all_to_all(outgoing, EXPERT, split_axis=0, concat_axis=0, tiled=True)
    own = local_kernel(
        functools.partial(arrange_kernel, capacity),
        jax.ShapeDtypeStruct((feature_width, slots), BF),
        4 * slots * slots * LANES,
        8 * slots * LANES,
    )(received.reshape(-1, LANES))
    other = swap(own)

    dense_saved, dense_down = after((dense_saved, dense_down), own)
    gate_dense, up_dense, sigmoid_dense, dense_units = swiglu_parts(dense_saved[0].T, dense_saved[1].T)
    dense_mine, dense_theirs = local_kernel(
        functools.partial(split_kernel, runs),
        [jax.ShapeDtypeStruct((hidden_count, model_width // 2), BF)] * 2,
        0,
        4 * hidden_count * model_width,
        1,
        1,
    )(half_index, dense_down)

    pair = in_order(own, after(other, (dense_units, dense_theirs)), 0).reshape(-1, slots)
    sent = gather_columns(pair)
    dense_units_other, dense_theirs = swap(after(dense_units, pair)), swap(after(dense_theirs, pair))

    grad_half = gather_columns(after(grad_rows, (pair, dense_mine, dense_units)))

    units = (jnp.where(first, dense_units, dense_units_other), jnp.where(first, dense_units_other, dense_units))
    block = (expert_count // 2, width + STACK, LANES)
    mine, theirs = local_kernel(
        functools.partial(terms_kernel, runs),
        [jax.ShapeDtypeStruct(block, F32), jax.ShapeDtypeStruct(block, BF)],
        2 * model_width * hidden_count * tokens,
        8 * model_width * LANES,
        1,
        3,
    )(core_index, grad_half, *after(units, (own, dense_theirs)))
    theirs = lax.ppermute(theirs, "core", [(0, 1), (1, 0)])

    pairs = local_kernel(
        pair_kernel, jax.ShapeDtypeStruct(block, BF), mine.size, 8 * mine.size, 0, 2
    )(mine, theirs)
    came = lax.all_to_all(pairs, ("zh", "x"), split_axis=0, concat_axis=0, tiled=True)
    expert_saved, expert_down = after((expert_saved, expert_down), pairs)
    gate_expert, up_expert, sigmoid_expert, expert_units = swiglu_parts(
        expert_saved[0, 0].T, expert_saved[0, 1].T
    )
    grad_half = after(grad_half, pairs)
    dense_other = jnp.einsum("hf,fr->hr", dense_theirs, grad_half, preferred_element_type=F32)
    dense_cot = jnp.einsum("hf,fr->hr", dense_mine, grad_half, preferred_element_type=F32)
    dense_cot = dense_cot + swap(dense_other.astype(BF)).astype(F32)
    dense_pre_grad = pre_cotangents(dense_cot, gate_dense, up_dense, sigmoid_dense).transpose(0, 2, 1)
    dense_share = scatter_total(came, width, hidden_count)
    sent = after(sent, (dense_pre_grad, dense_share, expert_units))
    expert_grad = jnp.einsum("hr,fr->hf", expert_units, sent, preferred_element_type=F32)
    expert_cot = jnp.einsum("hf,fr->hr", expert_down[0], sent, preferred_element_type=F32)
    expert_pre_grad = pre_cotangents(expert_cot, gate_expert, up_expert, sigmoid_expert)
    expert_pre_grad = expert_pre_grad.transpose(0, 2, 1)[None]
    expert_down_grad = expert_grad.astype(BF)[None]
    return (expert_pre_grad, expert_down_grad, dense_pre_grad, dense_share.T)


def solution(mesh):
    experts, tensors, pairs = mesh.devices.shape
    chips = min(8, experts // 2)
    fine = Mesh(
        mesh.devices.reshape(experts // (2 * chips), chips, 2, tensors, pairs),
        EXPERT + SHARE,
    )
    return jax.shard_map(
        body,
        mesh=fine,
        in_specs=(
            P(EXPERT, SHARE),
            P(EXPERT, None),
            P(EXPERT, None),
            P(EXPERT, SHARE, None),
            P(EXPERT, None, None, SHARE),
            P(SHARE, None),
            P(None, EXPERT, SHARE),
        ),
        out_specs=(
            P(EXPERT, None, None, SHARE),
            P(EXPERT, SHARE, None),
            P(None, EXPERT, SHARE),
            P(SHARE, EXPERT),
        ),
        check_vma=False,
    )
```

```python
import functools

import jax
import jax.numpy as jnp
from jax import lax
from jax.experimental import pallas as pl
from jax.experimental.pallas import tpu as pltpu
from jax.sharding import Mesh, PartitionSpec as P

BF = jnp.bfloat16
F32 = jnp.float32
EXPERT = ("zh", "x", "core")
SHARE = ("y", "zl")
LANES = 128
STACK = 16
VMEM_LIMIT = 48 * 1024 * 1024


def local_kernel(kernel, outs, flops, moved, scalars=0, arrays=1):
    specs = [pl.BlockSpec(memory_space=pltpu.SMEM)] * scalars
    return pl.pallas_call(
        kernel,
        out_shape=outs,
        in_specs=specs + [pl.BlockSpec(memory_space=pltpu.VMEM)] * arrays,
        compiler_params=pltpu.CompilerParams(vmem_limit_bytes=VMEM_LIMIT),
        cost_estimate=pl.CostEstimate(flops=flops, bytes_accessed=moved, transcendentals=0),
    )


def dispatch_kernel(experts, capacity, routes_in, probs_in, grad_in, out_ref, routes_ref, probs_ref, grad_ref, sems):
    copies = [
        pltpu.make_async_copy(routes_in, routes_ref, sems.at[0]),
        pltpu.make_async_copy(probs_in, probs_ref, sems.at[1]),
        pltpu.make_async_copy(grad_in, grad_ref, sems.at[2]),
    ]
    for copy in copies:
        copy.start()
    for copy in copies:
        copy.wait()
    tokens, features = routes_ref.shape[1], grad_ref.shape[0]
    rows = out_ref.shape[0]
    first, second = routes_ref[0:1, :], routes_ref[1:2, :]
    names = lax.broadcasted_iota(jnp.int32, (experts, tokens), 0)
    on_first, on_second = names == first, names == second
    named = (on_first | on_second).astype(F32).astype(BF)
    earlier = lax.broadcasted_iota(jnp.int32, (tokens, tokens), 0) < lax.broadcasted_iota(
        jnp.int32, (tokens, tokens), 1
    )
    before = jnp.dot(named, earlier.astype(F32).astype(BF), preferred_element_type=F32)
    place_first = jnp.sum(jnp.where(on_first, before, 0.0), axis=0, keepdims=True)
    place_second = jnp.sum(jnp.where(on_second, before, 0.0), axis=0, keepdims=True)
    slot_first = first * capacity + place_first.astype(jnp.int32)
    slot_second = second * capacity + place_second.astype(jnp.int32)
    step = rows // 4
    for part in range(4):
        row = lax.broadcasted_iota(jnp.int32, (step, 1), 0) + part * step
        slot = row // (2 * capacity) * capacity + row % capacity
        is_first, is_second = slot == slot_first, slot == slot_second
        table = jnp.where(is_first, probs_ref[0:1, :], jnp.where(is_second, probs_ref[1:2, :], 0.0))
        weight = jnp.sum(table, axis=1, keepdims=True)
        onehot = (is_first | is_second).astype(F32).astype(BF)
        picked = lax.dot_general(
            onehot, grad_ref[...], (((1,), (1,)), ((), ())), preferred_element_type=F32
        )
        sent = picked * weight
        low = sent[:, :LANES]
        high = jnp.concatenate(
            [sent[:, LANES:], jnp.zeros((step, 2 * LANES - features), F32)], axis=1
        )
        out_ref[part * step : (part + 1) * step, :] = jnp.where(
            row % (2 * capacity) < capacity, low, high
        ).astype(BF)


def arrange_kernel(capacity, came_ref, out_ref):
    rows, features, slots = came_ref.shape[0], out_ref.shape[0], out_ref.shape[1]
    parts = 2
    row_step, slot_step = rows // parts, slots // parts
    row = lax.broadcasted_iota(jnp.int32, (row_step, 1), 0)
    slot = lax.broadcasted_iota(jnp.int32, (1, slot_step), 1)
    wanted = slot // capacity * (2 * capacity) + slot % capacity
    for half in range(2):
        pick = (row == wanted + half * capacity).astype(F32).astype(BF)
        for part in range(parts):
            block = came_ref[part * row_step : (part + 1) * row_step, :]
            value = lax.dot_general(
                block, pick, (((0,), (0,)), ((), ())), preferred_element_type=F32
            ).astype(BF)
            top = min(features - half * LANES, LANES)
            out_ref[half * LANES : half * LANES + top, part * slot_step : (part + 1) * slot_step] = value[
                :top, :
            ]


def split_kernel(runs, half_ref, dense_ref, expert_ref, mine_ref, theirs_ref):
    width = dense_ref.shape[1] // (2 * runs)

    def columns(ref, half):
        return jnp.concatenate(
            [ref[:, (2 * run + half) * width : (2 * run + half + 1) * width] for run in range(runs)], axis=1
        )

    for half in range(2):

        @pl.when(half_ref[0] == half)
        def _():
            for index, ref in enumerate((dense_ref, expert_ref)):
                mine_ref[index] = columns(ref, half)
                theirs_ref[index] = columns(ref, 1 - half)


def join_kernel(runs, half_ref, own_ref, other_ref, out_ref):
    width = own_ref.shape[1] // runs

    def joined(low_ref, high_ref):
        pieces = []
        for run in range(runs):
            for ref in (low_ref, high_ref):
                pieces.append(ref[:, run * width : (run + 1) * width])
        return jnp.concatenate(pieces, axis=1)

    @pl.when(half_ref[0] == 0)
    def _():
        out_ref[...] = joined(own_ref, other_ref)

    @pl.when(half_ref[0] == 1)
    def _():
        out_ref[...] = joined(other_ref, own_ref)


def swiglu_parts(gate_saved, up_saved):
    gate_pre = gate_saved.astype(F32)
    up_pre = up_saved.astype(F32)
    sigmoid_gate = jax.nn.sigmoid(gate_pre)
    hidden = (gate_pre * sigmoid_gate * up_pre).astype(BF)
    return (gate_pre, up_pre, sigmoid_gate, hidden)


def pre_cotangents(hidden_cot, gate_pre, up_pre, sigmoid_gate):
    gate_cot = hidden_cot * up_pre * sigmoid_gate * (1.0 + gate_pre * (1.0 - sigmoid_gate))
    up_cot = hidden_cot * gate_pre * sigmoid_gate
    return jnp.stack([gate_cot, up_cot]).astype(BF)


def after(values, earlier):
    return lax.optimization_barrier((values, earlier))[0]


def swap(values):
    return lax.ppermute(values, "zl", [(0, 1), (1, 0)])


def gather_columns(rows):
    whole = lax.all_gather(rows, "y", axis=0, tiled=False)
    return whole.reshape(-1, rows.shape[1])


def terms_kernel(runs, core_ref, grad_ref, first_ref, second_ref, mine_ref, theirs_ref):
    pairs, rows, _ = mine_ref.shape
    hidden, width = first_ref.shape[0], rows - STACK
    span = pairs // runs
    extra, missing = hidden - LANES, -width % STACK
    for core in range(2):

        @pl.when(core_ref[0] == core)
        def _():
            for run in range(runs):
                grads = grad_ref[run * span * width : (run + 1) * span * width, :]
                for half, ref in enumerate((first_ref, second_ref)):
                    value = lax.dot_general(
                        grads, ref[...], (((1,), (1,)), ((), ())), preferred_element_type=F32
                    )
                    for index in range(span):
                        block = value[index * width : (index + 1) * width, :]
                        last = jnp.concatenate([block[:, LANES:], jnp.zeros((missing, extra), F32)], axis=0)
                        count = last.shape[0] // STACK
                        last = jnp.concatenate(
                            [last[piece * STACK : (piece + 1) * STACK, :] for piece in range(count)]
                            + [jnp.zeros((STACK, LANES - count * extra), F32)],
                            axis=1,
                        )
                        block = jnp.concatenate([block[:, :LANES], last], axis=0)
                        place = (run * 2 + half) * span + index
                        if place % 2 == core:
                            mine_ref[place // 2] = block
                        else:
                            theirs_ref[place // 2] = block.astype(BF)


def pair_kernel(mine_ref, other_ref, out_ref):
    out_ref[...] = (mine_ref[...] + other_ref[...].astype(F32)).astype(BF)


def total_kernel(came_ref, out_ref):
    parts, rows, _ = came_ref.shape
    width, hidden = out_ref.shape
    stack, extra = rows - width, hidden - LANES
    total = came_ref[0].astype(F32)
    for part in range(1, parts):
        total = total + came_ref[part].astype(F32)
    last = jnp.concatenate(
        [total[width:, piece * extra : (piece + 1) * extra] for piece in range(-(-width // stack))], axis=0
    )
    out_ref[...] = jnp.concatenate([total[:width, :], last[:width, :]], axis=1).astype(BF)


def scatter_total(came, width, hidden):
    mine = local_kernel(
        total_kernel, jax.ShapeDtypeStruct((width, hidden), BF), came.size, 2 * came.size
    )(came)
    chips = lax.axis_size("x")
    route = [(2 * x + z, 2 * (x ^ 2) + (1 - z)) for x in range(chips) for z in range(2)]
    other = lax.ppermute(mine, ("x", "zl"), route)
    here = lax.axis_index("x") // 2 % 2 == lax.axis_index("zl")
    return jnp.where(here, mine, other)


def body(grad_out, routes, probs, expert_down, expert_saved, dense_down, dense_saved):
    expert_count, runs = lax.axis_size(EXPERT), lax.axis_size("y")
    slots, hidden_count = expert_saved.shape[2:]
    capacity = slots // expert_count
    tokens, feature_width = grad_out.shape
    model_width = dense_down.shape[1]
    width = model_width // expert_count
    half = lax.axis_index("zl").astype(jnp.int32)
    half_index = half.reshape(1)
    core_index = lax.axis_index("core").astype(jnp.int32).reshape(1)
    first = half == 0
    grad_rows = grad_out.T

    outgoing = pl.pallas_call(
        functools.partial(dispatch_kernel, expert_count, capacity),
        out_shape=jax.ShapeDtypeStruct((expert_count * 2 * capacity, LANES), BF),
        in_specs=[pl.BlockSpec(memory_space=pl.ANY)] * 3,
        scratch_shapes=[
            pltpu.VMEM((2, tokens), jnp.int32),
            pltpu.VMEM((2, tokens), F32),
            pltpu.VMEM((feature_width, tokens), BF),
            pltpu.SemaphoreType.DMA((3,)),
        ],
        compiler_params=pltpu.CompilerParams(vmem_limit_bytes=VMEM_LIMIT),
        cost_estimate=pl.CostEstimate(
            flops=4 * slots * tokens * feature_width, bytes_accessed=4 * slots * LANES, transcendentals=0
        ),
    )(routes.T, probs.T, grad_rows)
    outgoing = outgoing.reshape(expert_count, 2 * capacity, LANES)
    received = lax.all_to_all(outgoing, EXPERT, split_axis=0, concat_axis=0, tiled=True)
    own = local_kernel(
        functools.partial(arrange_kernel, capacity),
        jax.ShapeDtypeStruct((feature_width, slots), BF),
        4 * slots * slots * LANES,
        8 * slots * LANES,
    )(received.reshape(-1, LANES))
    sent_half = gather_columns(own)

    dense_saved, expert_saved, dense_down, expert_down = after(
        (dense_saved, expert_saved, dense_down, expert_down), own
    )
    gate_dense, up_dense, sigmoid_dense, dense_units = swiglu_parts(dense_saved[0].T, dense_saved[1].T)
    gate_expert, up_expert, sigmoid_expert, expert_units = swiglu_parts(
        expert_saved[0, 0].T, expert_saved[0, 1].T
    )
    weights = jax.ShapeDtypeStruct((2, hidden_count, model_width // 2), BF)
    weights_mine, weights_theirs = local_kernel(
        functools.partial(split_kernel, runs), [weights, weights], 0, 8 * hidden_count * model_width, 1, 2
    )(half_index, dense_down, expert_down[0])
    both_units = jnp.concatenate([dense_units, expert_units], axis=1)
    units_other = swap(both_units)
    dense_units_other, expert_units_other = units_other[:, :tokens], units_other[:, tokens:]
    weights_swapped = swap(weights_theirs)

    grad_half = gather_columns(after(grad_rows, (own, both_units, weights_theirs)))

    units = (jnp.where(first, dense_units, dense_units_other), jnp.where(first, dense_units_other, dense_units))
    block = (expert_count // 2, width + STACK, LANES)
    mine, theirs = local_kernel(
        functools.partial(terms_kernel, runs),
        [jax.ShapeDtypeStruct(block, F32), jax.ShapeDtypeStruct(block, BF)],
        2 * model_width * hidden_count * tokens,
        8 * model_width * LANES,
        1,
        3,
    )(core_index, grad_half, *units)
    theirs = lax.ppermute(theirs, "core", [(0, 1), (1, 0)])

    pairs = local_kernel(
        pair_kernel, jax.ShapeDtypeStruct(block, BF), mine.size, 8 * mine.size, 0, 2
    )(mine, after(theirs, weights_swapped))
    came = lax.all_to_all(pairs, ("zh", "x"), split_axis=0, concat_axis=0, tiled=True)
    grad_half = after(grad_half, pairs)
    dense_other = jnp.einsum("hf,fr->hr", weights_swapped[0], grad_half, preferred_element_type=F32)
    dense_other = dense_other.astype(BF)
    dense_cot = jnp.einsum("hf,fr->hr", weights_mine[0], grad_half, preferred_element_type=F32)
    sent_half = after(sent_half, (dense_other, dense_cot))
    dense_other = swap(dense_other)

    grad_other = jnp.einsum("hr,fr->hf", expert_units_other, sent_half, preferred_element_type=F32)
    grad_other = grad_other.astype(BF)
    sent_half = after(sent_half, grad_other)
    grad_other = swap(grad_other)
    cot_other = jnp.einsum("hf,fr->hr", weights_swapped[1], sent_half, preferred_element_type=F32)
    cot_other = cot_other.astype(BF)
    sent_half, came, dense_other = after((sent_half, came, dense_other), cot_other)
    cot_other = swap(cot_other)
    grad_own = jnp.einsum("hr,fr->hf", expert_units, sent_half, preferred_element_type=F32).astype(BF)
    cot_own = jnp.einsum("hf,fr->hr", weights_mine[1], sent_half, preferred_element_type=F32)

    dense_share = scatter_total(came, width, hidden_count)
    dense_cot = dense_cot + dense_other.astype(F32)
    dense_pre_grad = pre_cotangents(dense_cot, gate_dense, up_dense, sigmoid_dense).transpose(0, 2, 1)
    expert_cot = cot_own + cot_other.astype(F32)
    expert_pre_grad = pre_cotangents(expert_cot, gate_expert, up_expert, sigmoid_expert)
    expert_down_grad = local_kernel(
        functools.partial(join_kernel, runs),
        jax.ShapeDtypeStruct((hidden_count, model_width), BF),
        0,
        4 * hidden_count * model_width,
        1,
        2,
    )(half_index, grad_own, grad_other)[None]
    expert_pre_grad = expert_pre_grad.transpose(0, 2, 1)[None]
    return (expert_pre_grad, expert_down_grad, dense_pre_grad, dense_share.T)


def solution(mesh):
    experts, tensors, pairs = mesh.devices.shape
    chips = min(8, experts // 2)
    fine = Mesh(
        mesh.devices.reshape(experts // (2 * chips), chips, 2, tensors, pairs),
        EXPERT + SHARE,
    )
    return jax.shard_map(
        body,
        mesh=fine,
        in_specs=(
            P(EXPERT, SHARE),
            P(EXPERT, None),
            P(EXPERT, None),
            P(EXPERT, SHARE, None),
            P(EXPERT, None, None, SHARE),
            P(SHARE, None),
            P(None, EXPERT, SHARE),
        ),
        out_specs=(
            P(EXPERT, None, None, SHARE),
            P(EXPERT, SHARE, None),
            P(None, EXPERT, SHARE),
            P(SHARE, EXPERT),
        ),
        check_vma=False,
    )
```

```python
import functools

import jax
import jax.numpy as jnp
from jax import lax
from jax.experimental import pallas as pl
from jax.experimental.pallas import tpu as pltpu
from jax.sharding import Mesh, PartitionSpec as P

BF = jnp.bfloat16
F32 = jnp.float32
EXPERT = ("zh", "x", "core")
SHARE = ("y", "zl")
LANES = 128
STACK = 16
VMEM_LIMIT = 48 * 1024 * 1024


def local_kernel(kernel, outs, flops, moved, scalars=0, arrays=1):
    specs = [pl.BlockSpec(memory_space=pltpu.SMEM)] * scalars
    return pl.pallas_call(
        kernel,
        out_shape=outs,
        in_specs=specs + [pl.BlockSpec(memory_space=pltpu.VMEM)] * arrays,
        compiler_params=pltpu.CompilerParams(vmem_limit_bytes=VMEM_LIMIT),
        cost_estimate=pl.CostEstimate(flops=flops, bytes_accessed=moved, transcendentals=0),
    )


def dispatch_kernel(experts, capacity, routes_in, probs_in, grad_in, out_ref, routes_ref, probs_ref, grad_ref, sems):
    copies = [
        pltpu.make_async_copy(routes_in, routes_ref, sems.at[0]),
        pltpu.make_async_copy(probs_in, probs_ref, sems.at[1]),
        pltpu.make_async_copy(grad_in, grad_ref, sems.at[2]),
    ]
    for copy in copies:
        copy.start()
    for copy in copies:
        copy.wait()
    tokens, features = routes_ref.shape[1], grad_ref.shape[0]
    rows = out_ref.shape[0]
    first, second = routes_ref[0:1, :], routes_ref[1:2, :]
    names = lax.broadcasted_iota(jnp.int32, (experts, tokens), 0)
    on_first, on_second = names == first, names == second
    named = (on_first | on_second).astype(F32).astype(BF)
    earlier = lax.broadcasted_iota(jnp.int32, (tokens, tokens), 0) < lax.broadcasted_iota(
        jnp.int32, (tokens, tokens), 1
    )
    before = jnp.dot(named, earlier.astype(F32).astype(BF), preferred_element_type=F32)
    place_first = jnp.sum(jnp.where(on_first, before, 0.0), axis=0, keepdims=True)
    place_second = jnp.sum(jnp.where(on_second, before, 0.0), axis=0, keepdims=True)
    slot_first = first * capacity + place_first.astype(jnp.int32)
    slot_second = second * capacity + place_second.astype(jnp.int32)
    step = rows // 4
    for part in range(4):
        row = lax.broadcasted_iota(jnp.int32, (step, 1), 0) + part * step
        slot = row // (2 * capacity) * capacity + row % capacity
        is_first, is_second = slot == slot_first, slot == slot_second
        table = jnp.where(is_first, probs_ref[0:1, :], jnp.where(is_second, probs_ref[1:2, :], 0.0))
        weight = jnp.sum(table, axis=1, keepdims=True)
        onehot = (is_first | is_second).astype(F32).astype(BF)
        picked = lax.dot_general(
            onehot, grad_ref[...], (((1,), (1,)), ((), ())), preferred_element_type=F32
        )
        sent = picked * weight
        low = sent[:, :LANES]
        high = jnp.concatenate(
            [sent[:, LANES:], jnp.zeros((step, 2 * LANES - features), F32)], axis=1
        )
        out_ref[part * step : (part + 1) * step, :] = jnp.where(
            row % (2 * capacity) < capacity, low, high
        ).astype(BF)


def arrange_kernel(capacity, came_ref, out_ref):
    rows, features, slots = came_ref.shape[0], out_ref.shape[0], out_ref.shape[1]
    parts = 2
    row_step, slot_step = rows // parts, slots // parts
    row = lax.broadcasted_iota(jnp.int32, (row_step, 1), 0)
    slot = lax.broadcasted_iota(jnp.int32, (1, slot_step), 1)
    wanted = slot // capacity * (2 * capacity) + slot % capacity
    for half in range(2):
        pick = (row == wanted + half * capacity).astype(F32).astype(BF)
        for part in range(parts):
            block = came_ref[part * row_step : (part + 1) * row_step, :]
            value = lax.dot_general(
                block, pick, (((0,), (0,)), ((), ())), preferred_element_type=F32
            ).astype(BF)
            top = min(features - half * LANES, LANES)
            out_ref[half * LANES : half * LANES + top, part * slot_step : (part + 1) * slot_step] = value[
                :top, :
            ]


def split_kernel(runs, half_ref, dense_ref, expert_ref, mine_ref, theirs_ref):
    width = dense_ref.shape[1] // (2 * runs)

    def columns(ref, half):
        return jnp.concatenate(
            [ref[:, (2 * run + half) * width : (2 * run + half + 1) * width] for run in range(runs)], axis=1
        )

    for half in range(2):

        @pl.when(half_ref[0] == half)
        def _():
            for index, ref in enumerate((dense_ref, expert_ref)):
                mine_ref[index] = columns(ref, half)
                theirs_ref[index] = columns(ref, 1 - half)


def join_kernel(runs, half_ref, own_ref, other_ref, out_ref):
    width = own_ref.shape[1] // runs

    def joined(low_ref, high_ref):
        pieces = []
        for run in range(runs):
            for ref in (low_ref, high_ref):
                pieces.append(ref[:, run * width : (run + 1) * width])
        return jnp.concatenate(pieces, axis=1)

    @pl.when(half_ref[0] == 0)
    def _():
        out_ref[...] = joined(own_ref, other_ref)

    @pl.when(half_ref[0] == 1)
    def _():
        out_ref[...] = joined(other_ref, own_ref)


def swiglu_parts(gate_saved, up_saved):
    gate_pre = gate_saved.astype(F32)
    up_pre = up_saved.astype(F32)
    sigmoid_gate = jax.nn.sigmoid(gate_pre)
    hidden = (gate_pre * sigmoid_gate * up_pre).astype(BF)
    return (gate_pre, up_pre, sigmoid_gate, hidden)


def pre_cotangents(hidden_cot, gate_pre, up_pre, sigmoid_gate):
    gate_cot = hidden_cot * up_pre * sigmoid_gate * (1.0 + gate_pre * (1.0 - sigmoid_gate))
    up_cot = hidden_cot * gate_pre * sigmoid_gate
    return jnp.stack([gate_cot, up_cot]).astype(BF)


def after(values, earlier):
    return lax.optimization_barrier((values, earlier))[0]


def swap(values):
    return lax.ppermute(values, "zl", [(0, 1), (1, 0)])


def gather_columns(rows):
    whole = lax.all_gather(rows, "y", axis=0, tiled=False)
    return whole.reshape(-1, rows.shape[1])


def terms_kernel(runs, core_ref, grad_ref, first_ref, second_ref, mine_ref, theirs_ref):
    pairs, rows, _ = mine_ref.shape
    hidden, width = first_ref.shape[0], rows - STACK
    span = pairs // runs
    extra, missing = hidden - LANES, -width % STACK
    for core in range(2):

        @pl.when(core_ref[0] == core)
        def _():
            for run in range(runs):
                grads = grad_ref[run * span * width : (run + 1) * span * width, :]
                for half, ref in enumerate((first_ref, second_ref)):
                    value = lax.dot_general(
                        grads, ref[...], (((1,), (1,)), ((), ())), preferred_element_type=F32
                    )
                    for index in range(span):
                        block = value[index * width : (index + 1) * width, :]
                        last = jnp.concatenate([block[:, LANES:], jnp.zeros((missing, extra), F32)], axis=0)
                        count = last.shape[0] // STACK
                        last = jnp.concatenate(
                            [last[piece * STACK : (piece + 1) * STACK, :] for piece in range(count)]
                            + [jnp.zeros((STACK, LANES - count * extra), F32)],
                            axis=1,
                        )
                        block = jnp.concatenate([block[:, :LANES], last], axis=0)
                        place = (run * 2 + half) * span + index
                        if place % 2 == core:
                            mine_ref[place // 2] = block
                        else:
                            theirs_ref[place // 2] = block.astype(BF)


def pair_kernel(mine_ref, other_ref, out_ref):
    out_ref[...] = (mine_ref[...] + other_ref[...].astype(F32)).astype(BF)


def total_kernel(came_ref, out_ref):
    parts, rows, _ = came_ref.shape
    width, hidden = out_ref.shape
    stack, extra = rows - width, hidden - LANES
    total = came_ref[0].astype(F32)
    for part in range(1, parts):
        total = total + came_ref[part].astype(F32)
    last = jnp.concatenate(
        [total[width:, piece * extra : (piece + 1) * extra] for piece in range(-(-width // stack))], axis=0
    )
    out_ref[...] = jnp.concatenate([total[:width, :], last[:width, :]], axis=1).astype(BF)


def scatter_total(came, width, hidden):
    mine = local_kernel(
        total_kernel, jax.ShapeDtypeStruct((width, hidden), BF), came.size, 2 * came.size
    )(came)
    chips = lax.axis_size("x")
    route = [(2 * x + z, 2 * (x ^ 2) + (1 - z)) for x in range(chips) for z in range(2)]
    other = lax.ppermute(mine, ("x", "zl"), route)
    here = lax.axis_index("x") // 2 % 2 == lax.axis_index("zl")
    return jnp.where(here, mine, other)


def body(grad_out, routes, probs, expert_down, expert_saved, dense_down, dense_saved):
    expert_count, runs = lax.axis_size(EXPERT), lax.axis_size("y")
    slots, hidden_count = expert_saved.shape[2:]
    capacity = slots // expert_count
    tokens, feature_width = grad_out.shape
    model_width = dense_down.shape[1]
    width = model_width // expert_count
    half = lax.axis_index("zl").astype(jnp.int32)
    half_index = half.reshape(1)
    core_index = lax.axis_index("core").astype(jnp.int32).reshape(1)
    first = half == 0
    grad_rows = grad_out.T

    outgoing = pl.pallas_call(
        functools.partial(dispatch_kernel, expert_count, capacity),
        out_shape=jax.ShapeDtypeStruct((expert_count * 2 * capacity, LANES), BF),
        in_specs=[pl.BlockSpec(memory_space=pl.ANY)] * 3,
        scratch_shapes=[
            pltpu.VMEM((2, tokens), jnp.int32),
            pltpu.VMEM((2, tokens), F32),
            pltpu.VMEM((feature_width, tokens), BF),
            pltpu.SemaphoreType.DMA((3,)),
        ],
        compiler_params=pltpu.CompilerParams(vmem_limit_bytes=VMEM_LIMIT),
        cost_estimate=pl.CostEstimate(
            flops=4 * slots * tokens * feature_width, bytes_accessed=4 * slots * LANES, transcendentals=0
        ),
    )(routes.T, probs.T, grad_rows)
    outgoing = outgoing.reshape(expert_count, 2 * capacity, LANES)
    received = lax.all_to_all(outgoing, EXPERT, split_axis=0, concat_axis=0, tiled=True)
    own = local_kernel(
        functools.partial(arrange_kernel, capacity),
        jax.ShapeDtypeStruct((feature_width, slots), BF),
        4 * slots * slots * LANES,
        8 * slots * LANES,
    )(received.reshape(-1, LANES))
    sent_half = gather_columns(own)

    dense_saved, expert_saved, dense_down, expert_down = after(
        (dense_saved, expert_saved, dense_down, expert_down), own
    )
    gate_dense, up_dense, sigmoid_dense, dense_units = swiglu_parts(dense_saved[0].T, dense_saved[1].T)
    gate_expert, up_expert, sigmoid_expert, expert_units = swiglu_parts(
        expert_saved[0, 0].T, expert_saved[0, 1].T
    )
    weights = jax.ShapeDtypeStruct((2, hidden_count, model_width // 2), BF)
    weights_mine, weights_theirs = local_kernel(
        functools.partial(split_kernel, runs), [weights, weights], 0, 8 * hidden_count * model_width, 1, 2
    )(half_index, dense_down, expert_down[0])
    both_units = jnp.concatenate([dense_units, expert_units], axis=1)
    units_other = swap(both_units)
    dense_units_other, expert_units_other = units_other[:, :tokens], units_other[:, tokens:]
    weights_swapped = swap(weights_theirs)

    grad_half = gather_columns(after(grad_rows, (own, both_units, weights_theirs)))

    units = (jnp.where(first, dense_units, dense_units_other), jnp.where(first, dense_units_other, dense_units))
    block = (expert_count // 2, width + STACK, LANES)
    mine, theirs = local_kernel(
        functools.partial(terms_kernel, runs),
        [jax.ShapeDtypeStruct(block, F32), jax.ShapeDtypeStruct(block, BF)],
        2 * model_width * hidden_count * tokens,
        8 * model_width * LANES,
        1,
        3,
    )(core_index, grad_half, *units)
    theirs = lax.ppermute(theirs, "core", [(0, 1), (1, 0)])

    pairs = local_kernel(
        pair_kernel, jax.ShapeDtypeStruct(block, BF), mine.size, 8 * mine.size, 0, 2
    )(mine, after(theirs, weights_swapped))
    came = lax.all_to_all(pairs, ("zh", "x"), split_axis=0, concat_axis=0, tiled=True)
    grad_half = after(grad_half, pairs)
    dense_other = jnp.einsum("hf,fr->hr", weights_swapped[0], grad_half, preferred_element_type=F32)
    dense_other = dense_other.astype(BF)
    dense_cot = jnp.einsum("hf,fr->hr", weights_mine[0], grad_half, preferred_element_type=F32)
    sent_half = after(sent_half, (dense_other, dense_cot))
    dense_other = swap(dense_other)

    cot_other = jnp.einsum("hf,fr->hr", weights_swapped[1], sent_half, preferred_element_type=F32)
    cot_other = cot_other.astype(BF)
    sent_half = after(sent_half, cot_other)
    cot_other = swap(cot_other)
    grad_other = jnp.einsum("hr,fr->hf", expert_units_other, sent_half, preferred_element_type=F32)
    grad_other = grad_other.astype(BF)
    sent_half, came, dense_other = after((sent_half, came, dense_other), grad_other)
    grad_other = swap(grad_other)
    grad_own = jnp.einsum("hr,fr->hf", expert_units, sent_half, preferred_element_type=F32).astype(BF)
    cot_own = jnp.einsum("hf,fr->hr", weights_mine[1], sent_half, preferred_element_type=F32)

    dense_share = scatter_total(came, width, hidden_count)
    dense_cot = dense_cot + dense_other.astype(F32)
    dense_pre_grad = pre_cotangents(dense_cot, gate_dense, up_dense, sigmoid_dense).transpose(0, 2, 1)
    expert_cot = cot_own + cot_other.astype(F32)
    expert_pre_grad = pre_cotangents(expert_cot, gate_expert, up_expert, sigmoid_expert)
    expert_down_grad = local_kernel(
        functools.partial(join_kernel, runs),
        jax.ShapeDtypeStruct((hidden_count, model_width), BF),
        0,
        4 * hidden_count * model_width,
        1,
        2,
    )(half_index, grad_own, grad_other)[None]
    expert_pre_grad = expert_pre_grad.transpose(0, 2, 1)[None]
    return (expert_pre_grad, expert_down_grad, dense_pre_grad, dense_share.T)


def solution(mesh):
    experts, tensors, pairs = mesh.devices.shape
    chips = min(8, experts // 2)
    fine = Mesh(
        mesh.devices.reshape(experts // (2 * chips), chips, 2, tensors, pairs),
        EXPERT + SHARE,
    )
    return jax.shard_map(
        body,
        mesh=fine,
        in_specs=(
            P(EXPERT, SHARE),
            P(EXPERT, None),
            P(EXPERT, None),
            P(EXPERT, SHARE, None),
            P(EXPERT, None, None, SHARE),
            P(SHARE, None),
            P(None, EXPERT, SHARE),
        ),
        out_specs=(
            P(EXPERT, None, None, SHARE),
            P(EXPERT, SHARE, None),
            P(None, EXPERT, SHARE),
            P(SHARE, EXPERT),
        ),
        check_vma=False,
    )
```
